32 devices in a mesh: groups: 2 (over y), ed: 4 (over z), dp: 2 (over x), tp: 2 (over core).
Axes of the slice: x: 2, y: 2, z: 4, core: 2. Of those that a mesh axis runs over, the one named last changes fastest.
Arguments:
- tokens: bfloat16 [1024, 2048], P(('groups', 'ed')), parts along dimension 0, may hold values from -6 to 6
- expert_ids: int32 [1024, 2], P(('groups', 'ed')), parts along dimension 0, may hold values from 0 to 7, all different within a row; in each aligned block of 128 rows (0 to 127, 128 to 255, ...) at most 48 rows name the same one
- gates: bfloat16 [1024, 2], P(('groups', 'ed')), parts along dimension 0, may hold values from 0.099609375 to 1
- out_grad: bfloat16 [1024, 2048], P(('groups', 'ed')), parts along dimension 0, may hold values from -6 to 6
- gate_weight: bfloat16 [2048, 57344], P(None, ('ed', 'dp', 'tp')), may hold values from -0.125 to 0.125
- up_weight: bfloat16 [2048, 57344], P(None, ('ed', 'dp', 'tp')), may hold values from -0.125 to 0.125
- down_weight: bfloat16 [57344, 2048], P(('ed', 'dp', 'tp')), may hold values from -0.0625 to 0.0625
Outputs:
- layer_out: bfloat16 [1024, 2048], P(('groups', 'ed')), parts along dimension 0
- token_grad: bfloat16 [1024, 2048], P(('groups', 'ed')), parts along dimension 0
- gate_grad: float32 [1024, 2], P(('groups', 'ed')), parts along dimension 0
- gate_weight_grad: bfloat16 [4096, 57344], P('groups', ('ed', 'dp', 'tp')), parts along dimension 0
- up_weight_grad: bfloat16 [4096, 57344], P('groups', ('ed', 'dp', 'tp')), parts along dimension 0
- down_weight_grad: bfloat16 [114688, 2048], P(('groups', 'ed', 'dp', 'tp')), parts along dimension 0
The draws below stay inside these ranges and needn't reach their ends.
There are 2 independent parts, one for each index of `groups`. The reference program is written for one: setup_inputs(seed, part) draws one part's arguments, and reference() takes and returns one part's arrays. A program takes and returns all parts, laid end to end along the dimension named above; an argument that names none is the same for every part. Nothing has to cross between parts.
Inputs may be any that keep to these rules, and one draw needn't show every extreme that they name: `expert_ids`: each row names 2 different experts. Among the 128 rows of one index of ed (aligned blocks of rows) no expert is named by more than 48 rows, and in every draw some expert is named by exactly 48 rows of some block.
All inputs are finite; a program needn't handle non-finite values.
Results may differ from the reference program's by a relative error of at most 0.0058.
Values may be sent and summed in bfloat16 or wider, within the bound.
No kernel may reach another device: no remote copies, remote signals or barrier semaphores. Data moves between devices by JAX's collectives and lax.ppermute only.
A program may use at most 192 MiB of HBM per device.

```python
import math
import jax
import jax.numpy as jnp
import numpy as np
from jax import lax

D = 2048
FF = 7168
EXPERTS = 8
TOP = 2
TOK_DEV = 128
CAP = 48
TOKENS = 512


def level_of(key, shape, shards, smallest, high):
    loudness, own = 1.0, jax.random.fold_in(key, 6)
    for axis_at, blocks in shards:
        steps = jnp.exp(jax.random.uniform(jax.random.fold_in(own, axis_at), (blocks,), jnp.float32, smallest / len(shards), high / len(shards)))
        loudness = loudness * jnp.repeat(steps, shape[axis_at] // blocks).reshape([-1 if axis == axis_at else 1 for axis in range(len(shape))])
    return loudness


def assign_block(stream_key, own, number, rows, amount, top, reach, lean):
    order = jax.random.permutation(stream_key, amount)
    packed, ordinary = load_shares(amount, rows * top, reach, lean, True), load_shares(amount, rows * top, reach, lean, False)
    places = jnp.arange(amount)

    def named(tallies, offset_by):
        used = int((tallies > 0).sum())
        fixed = max(1, used // 4)
        passed = fixed + (places - fixed + offset_by * (used - fixed)) % max(1, amount - fixed)
        return jnp.zeros((amount,), jnp.int32).at[order[jnp.where(places < fixed, places, passed)]].set(jnp.asarray(tallies, jnp.int32))

    tallies = jnp.where(number % 4 == 0, named(packed, number // 4), named(ordinary, number - number // 4 - 1))
    mixed = jax.random.permutation(jax.random.fold_in(own, 3), amount)
    source_of, receiver = mixed[0:amount // 2 * 2:2], mixed[1:amount // 2 * 2:2]
    margin = jnp.minimum(tallies[source_of] - 1, reach - tallies[receiver]) // 2
    margin = jnp.where((source_of == order[0]) | (receiver == order[0]) | (tallies[receiver] == 0), 0, jnp.maximum(margin, 0))
    passed = jax.random.randint(jax.random.fold_in(own, 4), (amount // 2,), 0, 1 << 20) % (margin + 1)
    tallies = tallies.at[source_of].add(-passed).at[receiver].add(passed)
    members = jnp.searchsorted(jnp.cumsum(tallies), jnp.arange(rows * top), side="right").astype(jnp.int32)
    grid = members.reshape(top, rows).T
    grid = grid[jax.random.permutation(jax.random.fold_in(own, 1), rows)]
    offset_by = jax.random.randint(jax.random.fold_in(own, 2), (rows, 1), 0, top)
    return jnp.take_along_axis(grid, (jnp.arange(top)[None, :] + offset_by) % top, axis=1)


def load_shares(count, total, reach, skew, full):
    weights = [(1 << 20) // math.isqrt(rank ** skew) + 1 for rank in range(1, count + 1)]
    largest = reach if full else min(reach, max(-(-total // count), total * weights[0] // sum(weights)))
    least = 1 if total - largest >= count - 1 else 0
    given, surplus = [largest] + [least] * (count - 1), total - largest - least * (count - 1)
    while surplus > 0:
        free = [i for i in range(1, count) if given[i] < largest] or [i for i in range(1, count) if given[i] < reach]
        whole, budget = sum([weights[i] for i in free]), surplus
        for i in free:
            more = min(reach - given[i], max(1, budget * weights[i] // whole), surplus)
            given[i] = given[i] + more
            surplus = surplus - more
    return np.array(given)


def gaussian(own_key, dims, width, most, split=(), kind=jnp.bfloat16):
    level = level_of(own_key, dims, split, -0.22, 0.18) if split else 1.0
    array = jax.random.normal(own_key, dims, jnp.float32) * width * level
    return jnp.minimum(jnp.maximum(array, -most), most).astype(kind)


def setup_inputs(seed: int = 0, part: int = 0) -> dict:
    seeds = jax.random.split(jax.random.key(seed), 8)
    part_keys = jax.random.split(jax.random.fold_in(seeds[7], part), 8)
    tokens = gaussian(part_keys[0], (TOKENS, D), 1.0, 6.0, ((0, 4),))
    expert_ids_keys = jax.random.split(jax.random.fold_in(part_keys[1], 1), TOKENS // TOK_DEV)
    expert_ids_turns = jax.random.permutation(jax.random.fold_in(part_keys[1], 3), TOKENS // TOK_DEV)
    expert_ids = jax.vmap(lambda own, number: assign_block(jax.random.fold_in(part_keys[1], 2), own, number, TOK_DEV, EXPERTS, TOP, CAP, 2))(expert_ids_keys, expert_ids_turns).reshape((TOKENS, TOP))
    gates = jnp.clip(0.099609375 + 0.9003906 * jax.random.uniform(part_keys[2], (TOKENS, TOP), jnp.float32) ** level_of(part_keys[2], (TOKENS, TOP), ((0, 4),), -0.2, 0.2), 0.099609375, 1.0).astype(jnp.bfloat16)
    out_grad = gaussian(part_keys[3], (TOKENS, D), 1.0, 6.0, ((0, 4),))
    gate_weight = gaussian(seeds[4], (D, EXPERTS * FF), D ** -0.5, 0.125, ((1, 16),))
    up_weight = gaussian(seeds[5], (D, EXPERTS * FF), D ** -0.5, 0.125, ((1, 16),))
    down_weight = gaussian(seeds[6], (EXPERTS * FF, D), FF ** -0.5, 0.0625, ((0, 16),))
    return {"tokens": tokens, "expert_ids": expert_ids, "gates": gates, "out_grad": out_grad, "gate_weight": gate_weight, "up_weight": up_weight, "down_weight": down_weight}


def contract_last(left_mat, right_mat):
    return lax.dot_general(left_mat, right_mat, (((1,), (1,)), ((), ())), preferred_element_type=jnp.float32)


def contract_first(left_mat, right_mat):
    return lax.dot_general(left_mat, right_mat, (((0,), (0,)), ((), ())), preferred_element_type=jnp.float32)


def expert_rows(rows_in, rows_grad, scale_col, gate_cols, up_cols, down_rows):
    pre_gate = jnp.dot(rows_in, gate_cols, preferred_element_type=jnp.float32)
    pre_up = jnp.dot(rows_in, up_cols, preferred_element_type=jnp.float32)
    logistic = jax.nn.sigmoid(pre_gate)
    silu_gate = pre_gate * logistic
    hidden = (silu_gate * pre_up).astype(jnp.bfloat16)
    partial_out = jnp.dot(hidden, down_rows, preferred_element_type=jnp.float32)
    back_rows = contract_last(rows_grad, down_rows)
    scale_two = scale_col[:, None]
    hidden_grad = scale_two * back_rows
    gate_pre_grad = (hidden_grad * pre_up * logistic * (1.0 + pre_gate * (1.0 - logistic))).astype(jnp.bfloat16)
    up_pre_grad = (hidden_grad * silu_gate).astype(jnp.bfloat16)
    partial_input = contract_last(gate_pre_grad, gate_cols) + contract_last(up_pre_grad, up_cols)
    out_scaled = (scale_two * rows_grad.astype(jnp.float32)).astype(jnp.bfloat16)
    grad_gate = contract_first(rows_in, gate_pre_grad)
    grad_up = contract_first(rows_in, up_pre_grad)
    grad_down = contract_first(hidden, out_scaled)
    return partial_out, partial_input, grad_gate, grad_up, grad_down


def reference(tokens, expert_ids, gates, out_grad, gate_weight, up_weight, down_weight):
    row_count = tokens.shape[0]
    slot_total = (row_count // TOK_DEV) * CAP
    positions = jnp.arange(slot_total, dtype=jnp.int32)
    layer_out = jnp.zeros((row_count, D), jnp.float32)
    token_grad = jnp.zeros((row_count, D), jnp.float32)
    gate_grad = jnp.zeros((row_count, TOP), jnp.float32)
    gate_parts = []
    up_parts = []
    down_parts = []
    for expert in range(EXPERTS):
        matches = expert_ids == expert
        chosen = jnp.any(matches, axis=1)
        weight_row = jnp.sum(jnp.where(matches, gates.astype(jnp.float32), jnp.zeros((), jnp.float32)), axis=1)
        picked = jnp.nonzero(chosen, size=slot_total, fill_value=0)[0].astype(jnp.int32)
        live_slot = positions < jnp.sum(chosen.astype(jnp.int32))
        scaled = jnp.where(live_slot, weight_row[picked], jnp.zeros((), jnp.float32))
        gate_cols = gate_weight[:, expert * FF:(expert + 1) * FF]
        up_cols = up_weight[:, expert * FF:(expert + 1) * FF]
        down_rows = down_weight[expert * FF:(expert + 1) * FF, :]
        rows_grad = out_grad[picked]
        partial_out, partial_input, grad_gate, grad_up, grad_down = expert_rows(
            tokens[picked], rows_grad, scaled, gate_cols, up_cols, down_rows)
        partial_gate = jnp.sum(partial_out * rows_grad.astype(jnp.float32), axis=1)
        layer_out = layer_out.at[picked].add(scaled[:, None] * partial_out)
        token_grad = token_grad.at[picked].add(partial_input)
        per_token = jnp.zeros((row_count,), jnp.float32).at[picked].add(
            jnp.where(live_slot, partial_gate, jnp.zeros((), jnp.float32)))
        gate_grad = gate_grad + jnp.where(matches, per_token[:, None], jnp.zeros((), jnp.float32))
        gate_parts.append(grad_gate.astype(jnp.bfloat16))
        up_parts.append(grad_up.astype(jnp.bfloat16))
        down_parts.append(grad_down.astype(jnp.bfloat16))
    return (layer_out.astype(jnp.bfloat16), token_grad.astype(jnp.bfloat16), gate_grad,
            jnp.concatenate(gate_parts, axis=1), jnp.concatenate(up_parts, axis=1),
            jnp.concatenate(down_parts, axis=0))
```

```python
import functools

import jax
import jax.numpy as jnp
from jax import lax
from jax.experimental import pallas as pl
from jax.experimental.pallas import tpu as pltpu
from jax.sharding import PartitionSpec as P

FF = 7168
CAP = 48
LANES = 128
F32 = jnp.float32
BF16 = jnp.bfloat16
VMEM_LIMIT = 56 * 1024 * 1024


def dot(left, right, left_dim=1, right_dim=0):
    return lax.dot_general(
        left, right, (((left_dim,), (right_dim,)), ((), ())), preferred_element_type=F32
    )


def params():
    return pltpu.CompilerParams(vmem_limit_bytes=VMEM_LIMIT)


def whole(shape):
    return pl.BlockSpec(shape, lambda *_: (0,) * len(shape))


def tile_of(size, most):
    for tile in (1024, 512, 256, 128):
        if tile <= most and size % tile == 0:
            return tile
    return size


def cost(flops, nbytes):
    return pl.CostEstimate(flops=int(flops), bytes_accessed=int(nbytes), transcendentals=0)


def shift(value, axis, step):
    count = lax.axis_size(axis)
    return lax.ppermute(value, axis, [(j, (j + step) % count) for j in range(count)])


def pick_body(n, half, scal, ids, gates, tokens, grads, *outs):
    tok_outs, grad_outs, coef_own, first, second, weighted = (
        outs[:n], outs[n:2 * n], outs[2 * n], outs[2 * n + 1], outs[2 * n + 2], outs[2 * n + 3],
    )
    rows = ids.shape[0]
    eye = (
        lax.broadcasted_iota(jnp.int32, (rows, rows), 0)
        == lax.broadcasted_iota(jnp.int32, (rows, rows), 1)
    ).astype(BF16)
    upper = (
        lax.broadcasted_iota(jnp.int32, (rows, rows), 0)
        <= lax.broadcasted_iota(jnp.int32, (rows, rows), 1)
    ).astype(BF16)
    ids_row = dot(ids[...].astype(F32).astype(BF16), eye, 0, 0)
    gates_row = dot(gates[...], eye, 0, 0)
    at = pl.multiple_of(scal[0] * half, half)
    slot_index = lax.broadcasted_iota(jnp.int32, (CAP, rows), 0).astype(F32)
    for s in range(n):
        expert = scal[1 + s].astype(F32)
        hit0 = (ids_row[0:1] == expert).astype(F32)
        hit1 = (ids_row[1:2] == expert).astype(F32)
        chosen = hit0 + hit1
        place = dot(jnp.broadcast_to(chosen, (8, rows)).astype(BF16), upper)[0:1] - 1.0
        here = (place == slot_index).astype(F32)
        placed0 = here * hit0
        placed1 = here * hit1
        weight = placed0 * gates_row[0:1] + placed1 * gates_row[1:2]
        placed = (placed0 + placed1).astype(BF16)
        span = pl.ds(s * CAP, CAP)
        first[span, :] = placed0.astype(BF16)
        second[span, :] = placed1.astype(BF16)
        weighted[span, :] = weight.astype(BF16)
        coef = jnp.broadcast_to(jnp.sum(weight, axis=1, keepdims=True), (CAP, LANES)).astype(BF16)
        if s == 0:
            tok_outs[0][...] = dot(placed, tokens[...]).astype(BF16)
            grad_outs[0][...] = dot(placed, grads[...]).astype(BF16)
            coef_own[...] = coef
        else:
            tok_outs[s][...] = dot(placed, tokens[:, pl.ds(at, half)]).astype(BF16)
            grad_outs[s][:, 0:half] = dot(placed, grads[:, pl.ds(at, half)]).astype(BF16)
            grad_outs[s][:, half:] = coef


def pick(n, scal, ids, gates, tokens, grads):
    rows, width = tokens.shape
    half = width // 2
    slots = n * CAP
    out = (
        [jax.ShapeDtypeStruct((CAP, width), BF16)]
        + [jax.ShapeDtypeStruct((CAP, half), BF16)] * (n - 1)
        + [jax.ShapeDtypeStruct((CAP, width), BF16)]
        + [jax.ShapeDtypeStruct((CAP, half + LANES), BF16)] * (n - 1)
        + [jax.ShapeDtypeStruct((CAP, LANES), BF16)]
        + [jax.ShapeDtypeStruct((slots, rows), BF16)] * 3
    )
    got = pl.pallas_call(
        functools.partial(pick_body, n, half),
        out_shape=out,
        grid_spec=pltpu.PrefetchScalarGridSpec(
            num_scalar_prefetch=1,
            grid=(1,),
            in_specs=[whole(v.shape) for v in (ids, gates, tokens, grads)],
            out_specs=[whole(v.shape) for v in out],
        ),
        compiler_params=params(),
        cost_estimate=cost(4 * slots * rows * width, 4 * rows * width * 2),
        name="pick",
    )(scal, ids, gates, tokens, grads)
    return got[:n], got[n:2 * n], got[2 * n], got[2 * n + 1:]


def gather_rows(n, half, scal, own, direct, other, held):
    mine = pl.multiple_of(scal[0] * half, half)
    theirs = pl.multiple_of((1 - scal[0]) * half, half)
    held[0:CAP, :] = own[...]
    for s in range(1, n):
        span = pl.ds(s * CAP, CAP)
        held[span, pl.ds(mine, half)] = direct[s - 1][:, 0:half]
        held[span, pl.ds(theirs, half)] = other[s - 1][:, 0:half]


def forward_body(n, half, scal, own, *refs):
    direct, other = refs[:n - 1], refs[n - 1:2 * n - 2]
    gate_w, up_w, rows_out, hidden, act, slope = refs[2 * n - 2:]

    @pl.when(pl.program_id(0) == 0)
    def _():
        gather_rows(n, half, scal, own, direct, other, rows_out)

    rows = rows_out[...]
    pre_gate = dot(rows, gate_w[...])
    pre_up = dot(rows, up_w[...])
    logistic = jax.nn.sigmoid(pre_gate)
    silu = pre_gate * logistic
    hidden[...] = (silu * pre_up).astype(BF16)
    act[...] = silu
    slope[...] = pre_up * logistic * (1.0 + pre_gate * (1.0 - logistic))


def forward(n, scal, own, direct, other, gate_w, up_w):
    width, hid = gate_w.shape
    slots = n * CAP
    tile = tile_of(hid, 512)
    column = lambda i, *_: (0, i)
    out = [
        jax.ShapeDtypeStruct((slots, width), BF16),
        jax.ShapeDtypeStruct((slots, hid), BF16),
        jax.ShapeDtypeStruct((slots, hid), F32),
        jax.ShapeDtypeStruct((slots, hid), F32),
    ]
    return pl.pallas_call(
        functools.partial(forward_body, n, width // 2),
        out_shape=out,
        grid_spec=pltpu.PrefetchScalarGridSpec(
            num_scalar_prefetch=1,
            grid=(hid // tile,),
            in_specs=[whole(v.shape) for v in (own, *direct, *other)]
            + [pl.BlockSpec((width, tile), column)] * 2,
            out_specs=[whole((slots, width))] + [pl.BlockSpec((slots, tile), column)] * 3,
        ),
        compiler_params=params(),
        cost_estimate=cost(4 * slots * width * hid, 4 * width * hid + 10 * slots * hid),
        name="forward",
    )(scal, own, *direct, *other, gate_w, up_w)


def middle_body(n, half, scal, own, coef_own, *refs):
    direct, other = refs[:n - 1], refs[n - 1:2 * n - 2]
    (hidden, act, slope, down, scaled, gate_grad, up_grad, send, keep, router,
     held, total, coef) = refs[2 * n - 2:]
    step = pl.program_id(0)

    @pl.when(step == 0)
    def _():
        gather_rows(n, half, scal, own, direct, other, held)
        coef[0:CAP, :] = coef_own[...].astype(F32)
        for s in range(1, n):
            coef[pl.ds(s * CAP, CAP), :] = direct[s - 1][:, half:].astype(F32)
        scaled[...] = (coef[:, 0:1] * held[...].astype(F32)).astype(BF16)
        router[...] = jnp.zeros_like(router)

    rows = hidden[...]
    back = dot(held[...], down[...], 1, 1)
    out = dot(rows, down[...])

    @pl.when(step == 0)
    def _():
        total[...] = out

    @pl.when(step > 0)
    def _():
        total[...] += out

    router[...] += jnp.broadcast_to(
        jnp.sum(rows.astype(F32) * back, axis=1, keepdims=True), router.shape
    )
    grad = coef[:, 0:1] * back
    gate_grad[...] = (grad * slope[...]).astype(BF16)
    up_grad[...] = (grad * act[...]).astype(BF16)

    @pl.when(step == pl.num_programs(0) - 1)
    def _():
        mine = pl.multiple_of(scal[0] * half, half)
        theirs = pl.multiple_of((1 - scal[0]) * half, half)
        send[...] = total[:, pl.ds(theirs, half)].astype(BF16)
        keep[...] = total[:, pl.ds(mine, half)]


def middle(n, scal, own, coef_own, direct, other, hidden, act, slope, down):
    hid, width = down.shape
    half = width // 2
    slots = n * CAP
    tile = tile_of(hid, 512)
    column = pl.BlockSpec((slots, tile), lambda i, *_: (0, i))
    out = [
        jax.ShapeDtypeStruct((slots, width), BF16),
        jax.ShapeDtypeStruct((slots, hid), BF16),
        jax.ShapeDtypeStruct((slots, hid), BF16),
        jax.ShapeDtypeStruct((slots, half), BF16),
        jax.ShapeDtypeStruct((slots, half), F32),
        jax.ShapeDtypeStruct((slots, LANES), F32),
    ]
    return pl.pallas_call(
        functools.partial(middle_body, n, half),
        out_shape=out,
        grid_spec=pltpu.PrefetchScalarGridSpec(
            num_scalar_prefetch=1,
            grid=(hid // tile,),
            in_specs=[whole(v.shape) for v in (own, coef_own, *direct, *other)]
            + [column] * 3
            + [pl.BlockSpec((tile, width), lambda i, *_: (i, 0))],
            out_specs=[whole((slots, width)), column, column]
            + [whole((slots, half)), whole((slots, half)), whole((slots, LANES))],
            scratch_shapes=[
                pltpu.VMEM((slots, width), BF16),
                pltpu.VMEM((slots, width), F32),
                pltpu.VMEM((slots, LANES), F32),
            ],
        ),
        compiler_params=params(),
        cost_estimate=cost(4 * slots * width * hid, 2 * width * hid + 14 * slots * hid),
        name="middle",
    )(scal, own, coef_own, *direct, *other, hidden, act, slope, down)


def backward_body(scal, gate_grad, up_grad, gate_w, up_w, out):
    out[...] = (
        dot(gate_grad[...], gate_w[...], 1, 1) + dot(up_grad[...], up_w[...], 1, 1)
    ).astype(out.dtype)


def backward(mine, kind, scal, gate_grad, up_grad, gate_w, up_w):
    width, hid = gate_w.shape
    half = width // 2
    slots = gate_grad.shape[0]
    tile = tile_of(half, 256)
    tiles = half // tile
    if mine:
        row = lambda i, scal: (scal[0] * tiles + i, 0)
    else:
        row = lambda i, scal: ((1 - scal[0]) * tiles + i, 0)
    return pl.pallas_call(
        backward_body,
        out_shape=jax.ShapeDtypeStruct((slots, half), kind),
        grid_spec=pltpu.PrefetchScalarGridSpec(
            num_scalar_prefetch=1,
            grid=(tiles,),
            in_specs=[whole((slots, hid))] * 2 + [pl.BlockSpec((tile, hid), row)] * 2,
            out_specs=pl.BlockSpec((slots, tile), lambda i, *_: (0, i)),
        ),
        compiler_params=params(),
        cost_estimate=cost(4 * slots * half * hid, 4 * half * hid),
        name="backward_keep" if mine else "backward_send",
    )(scal, gate_grad, up_grad, gate_w, up_w)


def columns_grad_body(rows, grad, out, flipped):
    @pl.when(pl.program_id(0) == 0)
    def _():
        flipped[...] = rows[...].T

    out[...] = dot(flipped[...], grad[...]).astype(BF16)


def columns_grad(rows, grad):
    slots, width = rows.shape
    hid = grad.shape[1]
    tile = tile_of(hid, 512)
    column = lambda i: (0, i)
    return pl.pallas_call(
        columns_grad_body,
        out_shape=jax.ShapeDtypeStruct((width, hid), BF16),
        grid=(hid // tile,),
        in_specs=[whole((slots, width)), pl.BlockSpec((slots, tile), column)],
        out_specs=pl.BlockSpec((width, tile), column),
        scratch_shapes=[pltpu.VMEM((width, slots), BF16)],
        compiler_params=params(),
        cost_estimate=cost(2 * slots * width * hid, 2 * width * hid),
        name="columns_grad",
    )(rows, grad)


def rows_grad_body(hidden, scaled, out):
    out[...] = dot(hidden[...], scaled[...], 0, 0).astype(BF16)


def rows_grad(hidden, scaled):
    slots, hid = hidden.shape
    width = scaled.shape[1]
    tile = tile_of(hid, 512)
    return pl.pallas_call(
        rows_grad_body,
        out_shape=jax.ShapeDtypeStruct((hid, width), BF16),
        grid=(hid // tile,),
        in_specs=[pl.BlockSpec((slots, tile), lambda i: (0, i)), whole((slots, width))],
        out_specs=pl.BlockSpec((tile, width), lambda i: (i, 0)),
        compiler_params=params(),
        cost_estimate=cost(2 * slots * width * hid, 2 * width * hid),
        name="rows_grad",
    )(hidden, scaled)


def three_parts(value):
    high = value.astype(BF16)
    rest = value - high.astype(F32)
    mid = rest.astype(BF16)
    return high, mid, (rest - mid.astype(F32)).astype(BF16)


def merge_body(n, keep, got, *refs):
    outs = refs[-n:]
    half = keep.shape[1]
    for s in range(n):
        span = pl.ds(s * CAP, CAP)
        outs[s][:, 0:half] = (keep[span, :] + got[span, :].astype(F32)).astype(BF16)
        if len(refs) > n:
            high, mid, low = three_parts(refs[0][span, :])
            lane = lax.broadcasted_iota(jnp.int32, (CAP, LANES), 1)
            outs[s][:, half:] = jnp.where(
                lane == 0, high, jnp.where(lane == 1, mid, jnp.where(lane == 2, low, jnp.zeros_like(low)))
            )


def merge(n, keep, got, router=None):
    half = keep.shape[1]
    wide = half + (0 if router is None else LANES)
    args = (keep, got) if router is None else (keep, got, router)
    return pl.pallas_call(
        functools.partial(merge_body, n),
        out_shape=[jax.ShapeDtypeStruct((CAP, wide), BF16)] * n,
        compiler_params=params(),
        cost_estimate=cost(0, 8 * keep.size),
        name="merge",
    )(*args)


def combine_body(n, weights, *refs):
    chunks, out = refs[:n], refs[-1]
    half = chunks[0].shape[1]
    total = dot(weights[0:CAP, :], chunks[0][...], 0, 0)
    for s in range(1, n):
        total += dot(weights[pl.ds(s * CAP, CAP), :], chunks[s][...], 0, 0)
    out[...] = total.astype(BF16)


def combine(n, weights, chunks):
    half = chunks[0].shape[1]
    return pl.pallas_call(
        functools.partial(combine_body, n),
        out_shape=jax.ShapeDtypeStruct((weights.shape[1], half), BF16),
        compiler_params=params(),
        cost_estimate=cost(2 * weights.size * half, 2 * n * CAP * half),
        name="combine",
    )(weights, *chunks)


def combine_router_body(n, half, first, second, *refs):
    chunks, out = refs[:n], refs[-1]
    rows = first.shape[1]
    total = jnp.zeros((rows, half), F32)
    score0 = jnp.zeros((rows, LANES), F32)
    score1 = jnp.zeros((rows, LANES), F32)
    for s in range(n):
        span = pl.ds(s * CAP, CAP)
        placed0, placed1 = first[span, :], second[span, :]
        total += dot(placed0 + placed1, chunks[s][:, 0:half], 0, 0)
        score0 += dot(placed0, chunks[s][:, half:], 0, 0)
        score1 += dot(placed1, chunks[s][:, half:], 0, 0)
    out[:, 0:half] = total.astype(BF16)
    out[:, half:] = spread_scores(
        jnp.sum(score0, axis=1, keepdims=True), jnp.sum(score1, axis=1, keepdims=True)
    )


def spread_scores(score0, score1):
    rows = score0.shape[0]
    lane = lax.broadcasted_iota(jnp.int32, (rows, LANES), 1)
    out = jnp.zeros((rows, LANES), F32)
    for k, score in enumerate((score0, score1)):
        for p, part in enumerate(three_parts(score)):
            out = jnp.where(lane == 3 * k + p, part.astype(F32), out)
    return out.astype(BF16)


def joined_scores(packed):
    values = packed.astype(F32)
    score0 = values[:, 0:1] + values[:, 1:2] + values[:, 2:3]
    score1 = values[:, 3:4] + values[:, 4:5] + values[:, 5:6]
    return score0, score1


def combine_router(n, first, second, chunks):
    wide = chunks[0].shape[1]
    rows = first.shape[1]
    return pl.pallas_call(
        functools.partial(combine_router_body, n, wide - LANES),
        out_shape=jax.ShapeDtypeStruct((rows, wide), BF16),
        compiler_params=params(),
        cost_estimate=cost(2 * first.size * wide, 2 * n * CAP * wide),
        name="combine_router",
    )(first, second, *chunks)


def add_body(half, *refs):
    pieces, out = refs[:-1], refs[-1]
    total = pieces[0][:, 0:half].astype(F32)
    for piece in pieces[1:]:
        total += piece[:, 0:half].astype(F32)
    out[:, 0:half] = total.astype(BF16)
    if out.shape[1] > half:
        score0, score1 = joined_scores(pieces[0][:, half:])
        for piece in pieces[1:]:
            more0, more1 = joined_scores(piece[:, half:])
            score0, score1 = score0 + more0, score1 + more1
        out[:, half:] = spread_scores(score0, score1)


def add_pieces(half, pieces):
    return pl.pallas_call(
        functools.partial(add_body, half),
        out_shape=jax.ShapeDtypeStruct(pieces[0].shape, BF16),
        compiler_params=params(),
        cost_estimate=cost(0, 6 * pieces[0].size),
        name="add_pieces",
    )(*pieces)


def finish_body(half, scal, own, other, out, *score):
    mine = pl.multiple_of(scal[0] * half, half)
    theirs = pl.multiple_of((1 - scal[0]) * half, half)
    out[:, pl.ds(mine, half)] = own[:, 0:half]
    out[:, pl.ds(theirs, half)] = other[:, 0:half]
    if score:
        own0, own1 = joined_scores(own[:, half:])
        other0, other1 = joined_scores(other[:, half:])
        lane = lax.broadcasted_iota(jnp.int32, score[0].shape, 1)
        score[0][...] = jnp.where(lane == 0, own0 + other0, own1 + other1)


def finish(half, scal, own, other):
    rows, wide = own.shape
    out = [jax.ShapeDtypeStruct((rows, 2 * half), BF16)]
    if wide > half:
        out.append(jax.ShapeDtypeStruct((rows, 2), F32))
    return pl.pallas_call(
        functools.partial(finish_body, half),
        out_shape=out,
        grid_spec=pltpu.PrefetchScalarGridSpec(
            num_scalar_prefetch=1,
            grid=(1,),
            in_specs=[whole(v.shape) for v in (own, other)],
            out_specs=[whole(v.shape) for v in out],
        ),
        compiler_params=params(),
        cost_estimate=cost(0, 4 * rows * wide),
        name="finish",
    )(scal, own, other)


def over_dp(half, value):
    count = lax.axis_size("dp")
    if count == 2:
        return add_pieces(half, [value, shift(value, "dp", 1)])
    gathered = lax.all_gather(value, "dp", axis=0, tiled=False)
    return add_pieces(half, [gathered[j] for j in range(count)])


def on_device(tokens, expert_ids, gates, out_grad, gate_weight, up_weight, down_weight):
    n = lax.axis_size("ed")
    reps = lax.axis_size(("dp", "tp"))
    me = lax.axis_index("ed")
    rep = lax.axis_index(("dp", "tp"))
    width = tokens.shape[1]
    half = width // 2
    hid = gate_weight.shape[1]
    owners = (me + jnp.arange(n, dtype=jnp.int32)) % n
    experts = (owners * reps + rep) * hid // FF
    scal = jnp.concatenate([lax.axis_index("tp").reshape(1), experts]).astype(jnp.int32)

    toks, grads, coef_own, (first, second, weighted) = pick(
        n, scal, expert_ids, gates, tokens, out_grad
    )
    tok_z = [shift(toks[s], "ed", s) for s in range(1, n)]
    grad_z = [shift(grads[s], "ed", s) for s in range(1, n)]
    tok_c = [shift(v, "tp", 1) for v in tok_z]
    rows, hidden, act, slope = forward(n, scal, toks[0], tok_z, tok_c, gate_weight, up_weight)
    grad_c = [shift(v, "tp", 1) for v in grad_z]
    scaled, gate_pre, up_pre, out_send, out_keep, router = middle(
        n, scal, grads[0], coef_own, grad_z, grad_c, hidden, act, slope, down_weight
    )
    out_got = shift(out_send, "tp", 1)
    in_send = backward(False, BF16, scal, gate_pre, up_pre, gate_weight, up_weight)
    out_chunks = merge(n, out_keep, out_got)
    out_back = [out_chunks[0]] + [shift(out_chunks[s], "ed", -s) for s in range(1, n)]
    in_got = shift(in_send, "tp", 1)
    in_keep = backward(True, F32, scal, gate_pre, up_pre, gate_weight, up_weight)
    in_chunks = merge(n, in_keep, in_got, router)
    in_back = [in_chunks[0]] + [shift(in_chunks[s], "ed", -s) for s in range(1, n)]
    down_grad = rows_grad(hidden, scaled)
    gate_w_grad = columns_grad(rows, gate_pre)
    up_w_grad = columns_grad(rows, up_pre)
    out_half = over_dp(half, combine(n, weighted, out_back))
    layer_out, = finish(half, scal, out_half, shift(out_half, "tp", 1))
    in_half = over_dp(half, combine_router(n, first, second, in_back))
    token_grad, gate_grad = finish(half, scal, in_half, shift(in_half, "tp", 1))
    return layer_out, token_grad, gate_grad, gate_w_grad, up_w_grad, down_grad


def solution(mesh):
    token_spec = P(("groups", "ed"), None)
    in_specs = (
        token_spec,
        token_spec,
        token_spec,
        token_spec,
        P(None, ("ed", "dp", "tp")),
        P(None, ("ed", "dp", "tp")),
        P(("ed", "dp", "tp"), None),
    )
    out_specs = (
        token_spec,
        token_spec,
        token_spec,
        P("groups", ("ed", "dp", "tp")),
        P("groups", ("ed", "dp", "tp")),
        P(("groups", "ed", "dp", "tp"), None),
    )
    return jax.shard_map(
        on_device, mesh=mesh, in_specs=in_specs, out_specs=out_specs, check_vma=False
    )
```

```python
import functools

import jax
import jax.numpy as jnp
from jax import lax
from jax.experimental import pallas as pl
from jax.experimental.pallas import tpu as pltpu
from jax.sharding import PartitionSpec as P

FF = 7168
CAP = 48
LANES = 128
F32 = jnp.float32
BF16 = jnp.bfloat16


def dot(left, right, left_dim=1, right_dim=0):
    return lax.dot_general(
        left, right, (((left_dim,), (right_dim,)), ((), ())), preferred_element_type=F32
    )


def params(megabytes=6, slots=0):
    scale = 1 if slots <= 256 else 4
    return pltpu.CompilerParams(vmem_limit_bytes=megabytes * scale * 1024 * 1024)


def tile_of(size, most):
    for tile in (1024, 512, 256):
        if tile <= most and size % tile == 0:
            return tile
    return size


def padded(slots):
    return -(-slots // 256) * 256


IN_VMEM = pl.BlockSpec(memory_space=pltpu.VMEM)
ANYWHERE = pl.BlockSpec(memory_space=pl.ANY)


def own_half(half):
    return pl.multiple_of(lax.axis_index("tp") * half, half)


def other_half(half):
    return pl.multiple_of((1 - lax.axis_index("tp")) * half, half)


def cost(flops, nbytes):
    return pl.CostEstimate(flops=int(flops), bytes_accessed=int(nbytes), transcendentals=0)


def shift(value, axis, step):
    count = lax.axis_size(axis)
    return lax.ppermute(value, axis, [(j, (j + step) % count) for j in range(count)])


def pick_tokens_body(n, hid, reps, ids, gates, tokens, *outs):
    toks, (first, second, weighted) = outs[:n], outs[n:]
    rows, width = tokens.shape
    half = width // 2
    upper = (
        lax.broadcasted_iota(jnp.int32, (rows, rows), 0)
        <= lax.broadcasted_iota(jnp.int32, (rows, rows), 1)
    ).astype(BF16)
    me, rep = lax.axis_index("ed"), lax.axis_index("dp") * 2 + lax.axis_index("tp")
    slot_index = lax.broadcasted_iota(jnp.int32, (CAP, rows), 0).astype(F32)
    gate0, gate1 = gates[0:1, :].astype(F32), gates[1:2, :].astype(F32)
    ids0, ids1 = ids[0:1, :], ids[1:2, :]
    for s in range(n):
        owner = lax.rem(me + s, n)
        expert = ((owner * reps + rep) * hid) // FF
        hit0 = jnp.where(ids0 == expert, 1.0, 0.0)
        hit1 = jnp.where(ids1 == expert, 1.0, 0.0)
        chosen = jnp.broadcast_to(hit0 + hit1, (8, rows)).astype(BF16)
        place = dot(chosen, upper)[0:1] - 1.0
        here = jnp.where(place == slot_index, 1.0, 0.0)
        placed0, placed1 = here * hit0, here * hit1
        placed = (placed0 + placed1).astype(BF16)
        span = pl.ds(s * CAP, CAP)
        first[span, :] = placed0.astype(BF16)
        second[span, :] = placed1.astype(BF16)
        weighted[span, :] = (placed0 * gate0 + placed1 * gate1).astype(BF16)
        if s == 0:
            toks[0][...] = dot(placed, tokens[...]).astype(BF16)
        else:
            toks[s][...] = dot(placed, tokens[:, pl.ds(own_half(half), half)]).astype(BF16)


def pick_tokens(n, hid, ids, gates, tokens):
    rows, width = tokens.shape
    slots = n * CAP
    out = (
        [jax.ShapeDtypeStruct((CAP, width), BF16)]
        + [jax.ShapeDtypeStruct((CAP, width // 2), BF16)] * (n - 1)
        + [jax.ShapeDtypeStruct((slots, rows), BF16)] * 3
    )
    got = pl.pallas_call(
        functools.partial(pick_tokens_body, n, hid, lax.axis_size(("dp", "tp"))),
        out_shape=out,
        compiler_params=params(),
        cost_estimate=cost(2 * slots * rows * width, 4 * rows * width),
        name="pick_tokens",
    )(ids, gates, tokens)
    return got[:n], got[n:]


def pick_grads_body(n, after, first, second, weighted, grads, *outs):
    half = grads.shape[1] // 2
    for s in range(n):
        span = pl.ds(s * CAP, CAP)
        placed = first[span, :] + second[span, :]
        coef = jnp.sum(weighted[span, :].astype(F32), axis=1, keepdims=True)
        coef = jnp.broadcast_to(coef, (CAP, LANES)).astype(BF16)
        if s == 0:
            outs[0][...] = dot(placed, grads[...]).astype(BF16)
            outs[n][...] = coef
        else:
            outs[s][:, 0:half] = dot(placed, grads[:, pl.ds(own_half(half), half)]).astype(BF16)
            outs[s][:, half:] = coef


def pick_grads(after, n, placing, grads):
    rows, width = grads.shape
    out = (
        [jax.ShapeDtypeStruct((CAP, width), BF16)]
        + [jax.ShapeDtypeStruct((CAP, width // 2 + LANES), BF16)] * (n - 1)
        + [jax.ShapeDtypeStruct((CAP, LANES), BF16)]
    )
    got = pl.pallas_call(
        functools.partial(pick_grads_body, n),
        out_shape=out,
        in_specs=[ANYWHERE] + [IN_VMEM] * 4,
        out_specs=[IN_VMEM] * (n + 1),
        compiler_params=params(),
        cost_estimate=cost(2 * n * CAP * rows * width, 4 * rows * width),
        name="pick_grads",
    )(after, *placing, grads)
    return got[:n], got[n]


def load_body(after, weight, held, done, sems):
    rows = weight.shape[0] // sems.shape[0]
    copies = [
        pltpu.make_async_copy(weight.at[pl.ds(j * rows, rows)], held.at[pl.ds(j * rows, rows)], sems.at[j])
        for j in range(sems.shape[0])
    ]
    for copy in copies:
        copy.start()
    done[...] = jnp.zeros_like(done)
    for copy in copies:
        copy.wait()


def load(after, weight):
    return pl.pallas_call(
        load_body,
        out_shape=[pltpu.VMEM(weight.shape, BF16), jax.ShapeDtypeStruct((8, LANES), F32)],
        in_specs=[ANYWHERE] * 2,
        out_specs=[IN_VMEM] * 2,
        scratch_shapes=[pltpu.SemaphoreType.DMA((4,))],
        compiler_params=params(1),
        cost_estimate=cost(0, 2 * weight.size),
        name="load",
    )(after, weight)


def stack_body(after, *refs):
    pieces, out = refs[:-1], refs[-1]
    for s, piece in enumerate(pieces):
        out[s * CAP:(s + 1) * CAP, :] = piece[...]


def stack(after, pieces):
    wide = pieces[0].shape[1]
    return pl.pallas_call(
        stack_body,
        out_shape=jax.ShapeDtypeStruct((len(pieces) * CAP, wide), BF16),
        in_specs=[ANYWHERE] + [IN_VMEM] * len(pieces),
        out_specs=IN_VMEM,
        compiler_params=params(),
        cost_estimate=cost(0, 4 * len(pieces) * CAP * wide),
        name="stack",
    )(after, *pieces)


def gather_rows(half, own, direct, other, held):
    held[0:CAP, :] = own[...]
    held[CAP:held.shape[0], pl.ds(own_half(half), half)] = direct[:, 0:half]
    held[CAP:held.shape[0], pl.ds(other_half(half), half)] = other[:, 0:half]


def clear_padding(slots, ref):
    if ref.shape[0] > slots:
        ref[slots:, :] = jnp.zeros((ref.shape[0] - slots, ref.shape[1]), ref.dtype)


def forward_body(slots, own, direct, other, gate_w, up_w, rows_out, hidden, act, slope):
    width, hid = gate_w.shape
    gather_rows(width // 2, own, direct, other, rows_out.at[pl.ds(0, slots)])
    clear_padding(slots, rows_out)
    clear_padding(slots, hidden)
    rows = rows_out[0:slots, :]
    tile = tile_of(hid, 512)
    for at in range(0, hid, tile):
        span = slice(at, at + tile)
        pre_gate = dot(rows, gate_w[:, span])
        pre_up = dot(rows, up_w[:, span])
        logistic = jax.nn.sigmoid(pre_gate)
        silu = pre_gate * logistic
        hidden[0:slots, span] = (silu * pre_up).astype(BF16)
        act[:, span] = silu.astype(BF16)
        slope[:, span] = (pre_up * logistic * (1.0 + pre_gate * (1.0 - logistic))).astype(BF16)


def forward(n, own, direct, other, gate_w, up_w):
    width, hid = gate_w.shape
    slots = n * CAP
    return pl.pallas_call(
        functools.partial(forward_body, slots),
        out_shape=[
            pltpu.VMEM((padded(slots), width), BF16),
            pltpu.VMEM((padded(slots), hid), BF16),
            pltpu.VMEM((slots, hid), BF16),
            pltpu.VMEM((slots, hid), BF16),
        ],
        in_specs=[IN_VMEM] * 5,
        out_specs=[IN_VMEM] * 4,
        compiler_params=params(6, slots),
        cost_estimate=cost(4 * slots * width * hid, 2 * slots * width),
        name="forward",
    )(own, direct, other, gate_w, up_w)


def streamed(down, buffers, sems, tile, columns):
    def copy(step):
        return pltpu.make_async_copy(
            down.at[pl.ds(step * tile, tile), columns],
            buffers.at[step % buffers.shape[0]],
            sems.at[step % buffers.shape[0]],
        )

    return copy


def expert_out_body(mine, slots, hidden, down, out, buffers, sems):
    hid, width = down.shape
    half = width // 2
    tile = buffers.shape[1]
    start = own_half(half) if mine else other_half(half)
    copy = streamed(down, buffers, sems, tile, pl.ds(start, half))
    steps = hid // tile
    depth = buffers.shape[0]
    for step in range(min(depth, steps)):
        copy(step).start()
    total = None
    for step in range(steps):
        copy(step).wait()
        part = dot(hidden[0:slots, step * tile:(step + 1) * tile], buffers[step % depth])
        total = part if total is None else total + part
        if step + depth < steps:
            copy(step + depth).start()
    out[...] = total.astype(out.dtype)


def expert_out(mine, kind, slots, hidden, down):
    hid, width = down.shape
    half = width // 2
    tile = tile_of(hid, 512)
    return pl.pallas_call(
        functools.partial(expert_out_body, mine, slots),
        out_shape=jax.ShapeDtypeStruct((slots, half), kind),
        in_specs=[IN_VMEM, ANYWHERE],
        out_specs=IN_VMEM,
        scratch_shapes=[pltpu.VMEM((4, tile, half), BF16), pltpu.SemaphoreType.DMA((4,))],
        compiler_params=params(8, slots),
        cost_estimate=cost(2 * slots * half * hid, 2 * half * hid),
        name="out_keep" if mine else "out_send",
    )(hidden, down)


def back_body(after, own, coef_own, direct, other, hidden, act, slope, down, scaled, gate_grad,
              up_grad, router, held, coef, buffers, sems):
    hid, width = down.shape
    half = width // 2
    slots = held.shape[0]
    depth, tile = buffers.shape[0:2]
    steps = hid // tile
    copy = streamed(down, buffers, sems, tile, slice(None))
    for step in range(min(depth, steps)):
        copy(step).start()
    gather_rows(half, own, direct, other, held)
    coef[0:CAP, :] = coef_own[...].astype(F32)
    coef[CAP:, :] = direct[:, half:].astype(F32)
    scale = coef[:, 0:1]
    scaled[0:slots, :] = (scale * held[...].astype(F32)).astype(BF16)
    for ref in (scaled, gate_grad, up_grad):
        clear_padding(slots, ref)
    score = None
    for step in range(steps):
        span = slice(step * tile, (step + 1) * tile)
        copy(step).wait()
        back = dot(held[...], buffers[step % depth], 1, 1)
        if step + depth < steps:
            copy(step + depth).start()
        part = jnp.sum(hidden[0:slots, span].astype(F32) * back, axis=1, keepdims=True)
        score = part if score is None else score + part
        grad = scale * back
        gate_grad[0:slots, span] = (grad * slope[:, span].astype(F32)).astype(BF16)
        up_grad[0:slots, span] = (grad * act[:, span].astype(F32)).astype(BF16)
    router[...] = jnp.broadcast_to(score, router.shape)


def back(after, n, own, coef_own, direct, other, hidden, act, slope, down):
    hid, width = down.shape
    slots = n * CAP
    tile = tile_of(hid, 256)
    return pl.pallas_call(
        back_body,
        out_shape=[
            pltpu.VMEM((padded(slots), width), BF16),
            pltpu.VMEM((padded(slots), hid), BF16),
            pltpu.VMEM((padded(slots), hid), BF16),
            jax.ShapeDtypeStruct((slots, LANES), F32),
        ],
        in_specs=[ANYWHERE] + [IN_VMEM] * 7 + [ANYWHERE],
        out_specs=[IN_VMEM] * 4,
        scratch_shapes=[
            pltpu.VMEM((slots, width), BF16),
            pltpu.VMEM((slots, LANES), F32),
            pltpu.VMEM((4, tile, width), BF16),
            pltpu.SemaphoreType.DMA((4,)),
        ],
        compiler_params=params(8, slots),
        cost_estimate=cost(2 * slots * width * hid, 2 * width * hid),
        name="back",
    )(after, own, coef_own, direct, other, hidden, act, slope, down)


def input_body(mine, gate_grad, up_grad, gate_w, up_w, out):
    slots, half = out.shape
    start = own_half(half) if mine else other_half(half)
    tile = tile_of(half, 256)
    for at in range(0, half, tile):
        span = pl.ds(start + at, tile)
        value = dot(gate_grad[0:slots, :], gate_w[span, :], 1, 1)
        value += dot(up_grad[0:slots, :], up_w[span, :], 1, 1)
        out[:, at:at + tile] = value.astype(out.dtype)


def input_part(mine, kind, slots, gate_grad, up_grad, gate_w, up_w):
    width, hid = gate_w.shape
    return pl.pallas_call(
        functools.partial(input_body, mine),
        out_shape=jax.ShapeDtypeStruct((slots, width // 2), kind),
        in_specs=[IN_VMEM] * 4,
        out_specs=IN_VMEM,
        compiler_params=params(6, slots),
        cost_estimate=cost(2 * slots * width * hid, 2 * slots * width),
        name="input_keep" if mine else "input_send",
    )(gate_grad, up_grad, gate_w, up_w)


def weight_grad_body(left, right, out, buffers, sems):
    depth, tile, columns = buffers.shape
    steps = out.shape[0] // tile
    piece = tile_of(columns, 512)

    def copy(step):
        slot = step % depth
        return pltpu.make_async_copy(
            buffers.at[slot], out.at[pl.ds(step * tile, tile), :], sems.at[slot]
        )

    for step in range(steps):
        flipped = left[:, step * tile:(step + 1) * tile].T
        if step >= depth:
            copy(step - depth).wait()
        for at in range(0, columns, piece):
            value = dot(flipped, right[:, at:at + piece])
            buffers[step % depth, :, at:at + piece] = value.astype(BF16)
        copy(step).start()
    for step in range(max(0, steps - depth), steps):
        copy(step).wait()


def weight_grad(left, right, name):
    slots, rows = left.shape
    columns = right.shape[1]
    tile = tile_of(rows, 256)
    return pl.pallas_call(
        weight_grad_body,
        out_shape=pltpu.HBM((rows, columns), BF16),
        in_specs=[IN_VMEM] * 2,
        out_specs=ANYWHERE,
        scratch_shapes=[pltpu.VMEM((4, tile, columns), BF16), pltpu.SemaphoreType.DMA((4,))],
        compiler_params=params(12, slots),
        cost_estimate=cost(2 * slots * rows * columns, 2 * rows * columns),
        name=name,
    )(left, right)


def three_parts(value):
    high = value.astype(BF16)
    rest = value - high.astype(F32)
    mid = rest.astype(BF16)
    return high, mid, (rest - mid.astype(F32)).astype(BF16)


def write_chunks(n, total, got, router, outs):
    half = total.shape[1]
    for s in range(n):
        span = slice(s * CAP, (s + 1) * CAP)
        outs[s][:, 0:half] = (total[span, :] + got[span, :].astype(F32)).astype(BF16)
        if router is not None:
            high, mid, low = three_parts(router[span, :])
            lane = lax.broadcasted_iota(jnp.int32, (CAP, LANES), 1)
            outs[s][:, half:] = jnp.where(
                lane == 0, high, jnp.where(lane == 1, mid, jnp.where(lane == 2, low, jnp.zeros_like(low)))
            )


def merge_body(n, keep, got, *refs):
    write_chunks(n, keep[...], got, refs[0] if len(refs) > n else None, refs[-n:])


def merge(n, keep, got, *router):
    wide = keep.shape[1] + LANES * len(router)
    return pl.pallas_call(
        functools.partial(merge_body, n),
        out_shape=[jax.ShapeDtypeStruct((CAP, wide), BF16)] * n,
        compiler_params=params(),
        cost_estimate=cost(0, 8 * keep.size),
        name="merge",
    )(keep, got, *router)


def combine_body(n, weights, *refs):
    chunks, out = refs[:n], refs[-1]
    half = chunks[0].shape[1]
    total = dot(weights[0:CAP, :], chunks[0][...], 0, 0)
    for s in range(1, n):
        total += dot(weights[pl.ds(s * CAP, CAP), :], chunks[s][...], 0, 0)
    out[...] = total.astype(BF16)


def combine(n, weights, chunks):
    half = chunks[0].shape[1]
    return pl.pallas_call(
        functools.partial(combine_body, n),
        out_shape=jax.ShapeDtypeStruct((weights.shape[1], half), BF16),
        compiler_params=params(),
        cost_estimate=cost(2 * weights.size * half, 2 * n * CAP * half),
        name="combine",
    )(weights, *chunks)


def combine_router_body(n, half, first, second, *refs):
    chunks, out = refs[:n], refs[-1]
    rows = first.shape[1]
    total = jnp.zeros((rows, half), F32)
    score0 = jnp.zeros((rows, LANES), F32)
    score1 = jnp.zeros((rows, LANES), F32)
    for s in range(n):
        span = pl.ds(s * CAP, CAP)
        placed0, placed1 = first[span, :], second[span, :]
        total += dot(placed0 + placed1, chunks[s][:, 0:half], 0, 0)
        score0 += dot(placed0, chunks[s][:, half:], 0, 0)
        score1 += dot(placed1, chunks[s][:, half:], 0, 0)
    out[:, 0:half] = total.astype(BF16)
    out[:, half:] = spread_scores(
        jnp.sum(score0, axis=1, keepdims=True), jnp.sum(score1, axis=1, keepdims=True)
    )


def spread_scores(score0, score1):
    rows = score0.shape[0]
    lane = lax.broadcasted_iota(jnp.int32, (rows, LANES), 1)
    out = jnp.zeros((rows, LANES), F32)
    for k, score in enumerate((score0, score1)):
        for p, part in enumerate(three_parts(score)):
            out = jnp.where(lane == 3 * k + p, part.astype(F32), out)
    return out.astype(BF16)


def joined_scores(packed):
    values = packed.astype(F32)
    score0 = values[:, 0:1] + values[:, 1:2] + values[:, 2:3]
    score1 = values[:, 3:4] + values[:, 4:5] + values[:, 5:6]
    return score0, score1


def combine_router(n, first, second, chunks):
    wide = chunks[0].shape[1]
    rows = first.shape[1]
    return pl.pallas_call(
        functools.partial(combine_router_body, n, wide - LANES),
        out_shape=jax.ShapeDtypeStruct((rows, wide), BF16),
        compiler_params=params(),
        cost_estimate=cost(2 * first.size * wide, 2 * n * CAP * wide),
        name="combine_router",
    )(first, second, *chunks)


def finish_body(half, count, *refs):
    own, other, out = refs[:count], refs[count:2 * count], refs[2 * count]
    for pieces, start in ((own, own_half(half)), (other, other_half(half))):
        total = pieces[0][:, 0:half].astype(F32)
        for piece in pieces[1:]:
            total += piece[:, 0:half].astype(F32)
        out[:, pl.ds(start, half)] = total.astype(BF16)
    if len(refs) > 2 * count + 1:
        scores = [[joined_scores(piece[:, half:]) for piece in pieces] for pieces in (own, other)]
        sums = [[sum(part[k] for part in parts) for k in range(2)] for parts in scores]
        lane = lax.broadcasted_iota(jnp.int32, refs[-1].shape, 1)
        refs[-1][...] = jnp.where(
            lane == 0, sums[0][0] + sums[1][0], sums[0][1] + sums[1][1]
        )


def finish(half, own, other):
    rows, wide = own[0].shape
    out = [jax.ShapeDtypeStruct((rows, 2 * half), BF16)]
    if wide > half:
        out.append(jax.ShapeDtypeStruct((rows, 2), F32))
    return pl.pallas_call(
        functools.partial(finish_body, half, len(own)),
        out_shape=out,
        compiler_params=params(),
        cost_estimate=cost(0, 4 * rows * wide),
        name="finish",
    )(*own, *other)


def over_chips(half, value):
    count = lax.axis_size("dp")
    if count == 2:
        own = [value, shift(value, "dp", 1)]
    else:
        gathered = lax.all_gather(value, "dp", axis=0, tiled=False)
        own = [gathered[j] for j in range(count)]
    return finish(half, own, [shift(piece, "tp", 1) for piece in own])


def on_device(tokens, expert_ids, gates, out_grad, gate_weight, up_weight, down_weight):
    ids, gates, tokens, out_grad, gate_weight, up_weight, down_weight = (
        pltpu.with_memory_space_constraint(v, pltpu.HBM)
        for v in (expert_ids.T, gates.T, tokens, out_grad, gate_weight, up_weight, down_weight)
    )
    n = lax.axis_size("ed")
    slots = n * CAP
    half = tokens.shape[1] // 2
    hid = gate_weight.shape[1]

    toks, placing = pick_tokens(n, hid, ids, gates, tokens)
    tok_z = [shift(toks[s], "ed", s) for s in range(1, n)]
    gate_held, gate_done = load(toks[0], gate_weight)
    grads, coef_own = pick_grads(gate_done, n, placing, out_grad)
    grad_z = [shift(grads[s], "ed", s) for s in range(1, n)]
    up_held, up_done = load(grads[0], up_weight)
    tok_all = stack(up_done, tok_z)
    rows, hidden, act, slope = forward(
        n, toks[0], tok_all, shift(tok_all, "tp", 1), gate_held, up_held
    )
    out_part = expert_out(False, BF16, slots, hidden, down_weight)
    out_got = shift(out_part, "tp", 1)
    out_keep = expert_out(True, F32, slots, hidden, down_weight)
    out_chunks = merge(n, out_keep, out_got)
    out_back = [out_chunks[0]] + [shift(out_chunks[s], "ed", -s) for s in range(1, n)]
    grad_all = stack(hidden, grad_z)
    scaled, gate_pre, up_pre, router = back(
        out_chunks[0], n, grads[0], coef_own, grad_all, shift(grad_all, "tp", 1),
        hidden, act, slope, down_weight,
    )
    in_part = input_part(False, BF16, slots, gate_pre, up_pre, gate_held, up_held)
    in_got = shift(in_part, "tp", 1)
    in_keep = input_part(True, F32, slots, gate_pre, up_pre, gate_held, up_held)
    in_chunks = merge(n, in_keep, in_got, router)
    in_back = [in_chunks[0]] + [shift(in_chunks[s], "ed", -s) for s in range(1, n)]
    down_grad = weight_grad(hidden, scaled, "down_grad")
    gate_w_grad = weight_grad(rows, gate_pre, "gate_grad")
    up_w_grad = weight_grad(rows, up_pre, "up_grad")
    first, second, weighted = placing
    layer_out, = over_chips(half, combine(n, weighted, out_back))
    token_grad, gate_grad = over_chips(half, combine_router(n, first, second, in_back))
    return layer_out, token_grad, gate_grad, gate_w_grad, up_w_grad, down_grad


def solution(mesh):
    token_spec = P(("groups", "ed"), None)
    in_specs = (
        token_spec,
        token_spec,
        token_spec,
        token_spec,
        P(None, ("ed", "dp", "tp")),
        P(None, ("ed", "dp", "tp")),
        P(("ed", "dp", "tp"), None),
    )
    out_specs = (
        token_spec,
        token_spec,
        token_spec,
        P("groups", ("ed", "dp", "tp")),
        P("groups", ("ed", "dp", "tp")),
        P(("groups", "ed", "dp", "tp"), None),
    )
    return jax.shard_map(
        on_device, mesh=mesh, in_specs=in_specs, out_specs=out_specs, check_vma=False
    )
```

```python
import functools

import jax
import jax.numpy as jnp
from jax import lax
from jax.experimental import pallas as pl
from jax.experimental.pallas import tpu as pltpu
from jax.sharding import PartitionSpec as P

FF = 7168
CAP = 48
LANES = 128
F32 = jnp.float32
BF16 = jnp.bfloat16


def dot(left, right, left_dim=1, right_dim=0):
    return lax.dot_general(
        left, right, (((left_dim,), (right_dim,)), ((), ())), preferred_element_type=F32
    )


def params(megabytes=6, slots=0):
    scale = 1 if slots <= 256 else 4
    return pltpu.CompilerParams(vmem_limit_bytes=megabytes * scale * 1024 * 1024)


def tile_of(size, most):
    for tile in (1024, 512, 256):
        if tile <= most and size % tile == 0:
            return tile
    return size


def padded(slots):
    return -(-slots // 256) * 256


IN_VMEM = pl.BlockSpec(memory_space=pltpu.VMEM)
ANYWHERE = pl.BlockSpec(memory_space=pl.ANY)


def own_half(half):
    return pl.multiple_of(lax.axis_index("tp") * half, half)


def other_half(half):
    return pl.multiple_of((1 - lax.axis_index("tp")) * half, half)


def cost(flops, nbytes):
    return pl.CostEstimate(flops=int(flops), bytes_accessed=int(nbytes), transcendentals=0)


def shift(value, axis, step):
    count = lax.axis_size(axis)
    return lax.ppermute(value, axis, [(j, (j + step) % count) for j in range(count)])


def pick_body(n, hid, reps, ids, gates, tokens, grads, *outs):
    own_tok, own_grad, own_coef = outs[0:3]
    first, second, weighted = outs[n + 2:]
    rows, width = tokens.shape
    half = width // 2
    upper = (
        lax.broadcasted_iota(jnp.int32, (rows, rows), 0)
        <= lax.broadcasted_iota(jnp.int32, (rows, rows), 1)
    ).astype(BF16)
    me, rep = lax.axis_index("ed"), lax.axis_index("dp") * 2 + lax.axis_index("tp")
    slot_index = lax.broadcasted_iota(jnp.int32, (CAP, rows), 0).astype(F32)
    gate0, gate1 = gates[0:1, :].astype(F32), gates[1:2, :].astype(F32)
    ids0, ids1 = ids[0:1, :], ids[1:2, :]
    for s in range(n):
        owner = lax.rem(me + s, n)
        expert = ((owner * reps + rep) * hid) // FF
        hit0 = jnp.where(ids0 == expert, 1.0, 0.0)
        hit1 = jnp.where(ids1 == expert, 1.0, 0.0)
        chosen = jnp.broadcast_to(hit0 + hit1, (8, rows)).astype(BF16)
        place = dot(chosen, upper)[0:1] - 1.0
        here = jnp.where(place == slot_index, 1.0, 0.0)
        placed0, placed1 = here * hit0, here * hit1
        placed = (placed0 + placed1).astype(BF16)
        weight = placed0 * gate0 + placed1 * gate1
        span = pl.ds(s * CAP, CAP)
        first[span, :] = placed0.astype(BF16)
        second[span, :] = placed1.astype(BF16)
        weighted[span, :] = weight.astype(BF16)
        coef = jnp.broadcast_to(jnp.sum(weight, axis=1, keepdims=True), (CAP, LANES)).astype(BF16)
        if s == 0:
            own_tok[...] = dot(placed, tokens[...]).astype(BF16)
            own_grad[...] = dot(placed, grads[...]).astype(BF16)
            own_coef[...] = coef
        else:
            mine = pl.ds(own_half(half), half)
            out = outs[2 + s]
            out[:, 0:half] = dot(placed, tokens[:, mine]).astype(BF16)
            out[:, half:width] = dot(placed, grads[:, mine]).astype(BF16)
            out[:, width:] = coef


def pick(n, hid, ids, gates, tokens, grads):
    rows, width = tokens.shape
    slots = n * CAP
    out = (
        [jax.ShapeDtypeStruct((CAP, width), BF16)] * 2
        + [jax.ShapeDtypeStruct((CAP, LANES), BF16)]
        + [jax.ShapeDtypeStruct((CAP, width + LANES), BF16)] * (n - 1)
        + [jax.ShapeDtypeStruct((slots, rows), BF16)] * 3
    )
    got = pl.pallas_call(
        functools.partial(pick_body, n, hid, lax.axis_size(("dp", "tp"))),
        out_shape=out,
        compiler_params=params(),
        cost_estimate=cost(4 * slots * rows * width, 8 * rows * width),
        name="pick",
    )(ids, gates, tokens, grads)
    return got[0:3], got[3:n + 2], got[n + 2:]


def load_body(after, weight, held, done, sems):
    rows = weight.shape[0] // sems.shape[0]
    copies = [
        pltpu.make_async_copy(weight.at[pl.ds(j * rows, rows)], held.at[pl.ds(j * rows, rows)], sems.at[j])
        for j in range(sems.shape[0])
    ]
    for copy in copies:
        copy.start()
    done[...] = jnp.zeros_like(done)
    for copy in copies:
        copy.wait()


def load(after, weight):
    return pl.pallas_call(
        load_body,
        out_shape=[pltpu.VMEM(weight.shape, BF16), jax.ShapeDtypeStruct((8, LANES), F32)],
        in_specs=[ANYWHERE] * 2,
        out_specs=[IN_VMEM] * 2,
        scratch_shapes=[pltpu.SemaphoreType.DMA((4,))],
        compiler_params=params(19),
        cost_estimate=cost(0, 2 * LANES),
        name="load",
    )(after, weight)


def stack_body(after, *refs):
    pieces, out = refs[:-1], refs[-1]
    for s, piece in enumerate(pieces):
        out[s * CAP:(s + 1) * CAP, :] = piece[...]


def stack(after, pieces):
    wide = pieces[0].shape[1]
    return pl.pallas_call(
        stack_body,
        out_shape=jax.ShapeDtypeStruct((len(pieces) * CAP, wide), BF16),
        in_specs=[ANYWHERE] + [IN_VMEM] * len(pieces),
        out_specs=IN_VMEM,
        compiler_params=params(),
        cost_estimate=cost(0, 4 * len(pieces) * CAP * wide),
        name="stack",
    )(after, *pieces)


def gather_rows(half, at, own, direct, other, held):
    held[0:CAP, :] = own[...]
    held[CAP:held.shape[0], pl.ds(own_half(half), half)] = direct[:, at:at + half]
    held[CAP:held.shape[0], pl.ds(other_half(half), half)] = other[:, at:at + half]


def clear_padding(slots, ref):
    if ref.shape[0] > slots:
        ref[slots:, :] = jnp.zeros((ref.shape[0] - slots, ref.shape[1]), ref.dtype)


def forward_body(slots, own, direct, other, gate_w, up_w, rows_out, hidden, act, slope):
    width, hid = gate_w.shape
    gather_rows(width // 2, 0, own, direct, other, rows_out.at[pl.ds(0, slots)])
    clear_padding(slots, rows_out)
    clear_padding(slots, hidden)
    rows = rows_out[0:slots, :]
    tile = tile_of(hid, 512)
    for at in range(0, hid, tile):
        span = slice(at, at + tile)
        pre_gate = dot(rows, gate_w[:, span])
        pre_up = dot(rows, up_w[:, span])
        logistic = jax.nn.sigmoid(pre_gate)
        silu = pre_gate * logistic
        hidden[0:slots, span] = (silu * pre_up).astype(BF16)
        act[:, span] = silu.astype(BF16)
        slope[:, span] = (pre_up * logistic * (1.0 + pre_gate * (1.0 - logistic))).astype(BF16)


def forward(n, own, direct, other, gate_w, up_w):
    width, hid = gate_w.shape
    slots = n * CAP
    return pl.pallas_call(
        functools.partial(forward_body, slots),
        out_shape=[
            pltpu.VMEM((padded(slots), width), BF16),
            pltpu.VMEM((padded(slots), hid), BF16),
            pltpu.VMEM((slots, hid), BF16),
            pltpu.VMEM((slots, hid), BF16),
        ],
        in_specs=[IN_VMEM] * 5,
        out_specs=[IN_VMEM] * 4,
        compiler_params=params(6, slots),
        cost_estimate=cost(0, 2 * slots * width),
        name="forward",
    )(own, direct, other, gate_w, up_w)


def streamed(down, buffers, sems, tile, columns):
    def copy(step):
        return pltpu.make_async_copy(
            down.at[pl.ds(step * tile, tile), columns],
            buffers.at[step % buffers.shape[0]],
            sems.at[step % buffers.shape[0]],
        )

    return copy


def middle_body(own, coef_own, direct, other, hidden, act, slope, down, scaled, gate_grad,
                up_grad, router, send, keep, held, total, coef, buffers, sems):
    hid, width = down.shape
    half = width // 2
    slots = held.shape[0]
    depth, tile = buffers.shape[0:2]
    steps = hid // tile
    copy = streamed(down, buffers, sems, tile, slice(None))
    for step in range(min(depth, steps)):
        copy(step).start()
    gather_rows(half, half, own, direct, other, held)
    coef[0:CAP, :] = coef_own[...].astype(F32)
    coef[CAP:, :] = direct[:, width:].astype(F32)
    scale = coef[:, 0:1]
    for ref in (scaled, gate_grad, up_grad):
        clear_padding(slots, ref)
    scaled[0:slots, :] = (scale * held[...].astype(F32)).astype(BF16)
    score = jnp.zeros((slots, LANES), F32)
    for step in range(steps):
        span = slice(step * tile, (step + 1) * tile)
        copy(step).wait()
        weight = buffers[step % depth]
        rows = hidden[0:slots, span]
        back = dot(held[...], weight, 1, 1)
        for at in range(0, width, half):
            part = dot(rows, buffers[step % depth, :, at:at + half])
            if step:
                total[:, at:at + half] += part
            else:
                total[:, at:at + half] = part
        if step + depth < steps:
            copy(step + depth).start()
        product = rows.astype(F32) * back
        for lane in range(0, tile // LANES * LANES, LANES):
            score += product[:, lane:lane + LANES]
        if tile % LANES:
            rest = jnp.sum(product[:, tile // LANES * LANES:], axis=1, keepdims=True)
            score += jnp.where(lax.broadcasted_iota(jnp.int32, score.shape, 1) == 0, rest, 0.0)
        grad = scale * back
        gate_grad[0:slots, span] = (grad * slope[:, span].astype(F32)).astype(BF16)
        up_grad[0:slots, span] = (grad * act[:, span].astype(F32)).astype(BF16)
    send[...] = total[:, pl.ds(other_half(half), half)].astype(BF16)
    keep[...] = total[:, pl.ds(own_half(half), half)]
    router[...] = jnp.broadcast_to(jnp.sum(score, axis=1, keepdims=True), router.shape)


def middle(n, own, coef_own, direct, other, hidden, act, slope, down):
    hid, width = down.shape
    half = width // 2
    slots = n * CAP
    tile = tile_of(hid, 256)
    return pl.pallas_call(
        middle_body,
        out_shape=[
            pltpu.VMEM((padded(slots), width), BF16),
            pltpu.VMEM((padded(slots), hid), BF16),
            pltpu.VMEM((padded(slots), hid), BF16),
            jax.ShapeDtypeStruct((slots, LANES), F32),
            jax.ShapeDtypeStruct((slots, half), BF16),
            jax.ShapeDtypeStruct((slots, half), F32),
        ],
        in_specs=[IN_VMEM] * 7 + [ANYWHERE],
        out_specs=[IN_VMEM] * 6,
        scratch_shapes=[
            pltpu.VMEM((slots, width), BF16),
            pltpu.VMEM((slots, width), F32),
            pltpu.VMEM((slots, LANES), F32),
            pltpu.VMEM((2, tile, width), BF16),
            pltpu.SemaphoreType.DMA((2,)),
        ],
        compiler_params=params(7, slots),
        cost_estimate=cost(4 * slots * width * hid, 2 * width * hid),
        name="middle",
    )(own, coef_own, direct, other, hidden, act, slope, down)


def input_body(mine, gate_grad, up_grad, gate_w, up_w, out):
    slots, half = out.shape
    start = own_half(half) if mine else other_half(half)
    tile = tile_of(half, 256)
    for at in range(0, half, tile):
        span = pl.ds(start + at, tile)
        value = dot(gate_grad[0:slots, :], gate_w[span, :], 1, 1)
        value += dot(up_grad[0:slots, :], up_w[span, :], 1, 1)
        out[:, at:at + tile] = value.astype(out.dtype)


def input_part(mine, kind, slots, gate_grad, up_grad, gate_w, up_w):
    width, hid = gate_w.shape
    return pl.pallas_call(
        functools.partial(input_body, mine),
        out_shape=jax.ShapeDtypeStruct((slots, width // 2), kind),
        in_specs=[IN_VMEM] * 4,
        out_specs=IN_VMEM,
        compiler_params=params(6, slots),
        cost_estimate=cost(2 * slots * width * hid, 2 * slots * width),
        name="input_keep" if mine else "input_send",
    )(gate_grad, up_grad, gate_w, up_w)


def weight_grad_body(after, left, right, out, done, buffers, sems):
    done[...] = jnp.zeros_like(done)
    depth, tile, columns = buffers.shape
    steps = out.shape[0] // tile
    piece = tile_of(columns, 512)

    def copy(step):
        slot = step % depth
        return pltpu.make_async_copy(
            buffers.at[slot], out.at[pl.ds(step * tile, tile), :], sems.at[slot]
        )

    for step in range(steps):
        flipped = left[:, step * tile:(step + 1) * tile].T
        if step >= depth:
            copy(step - depth).wait()
        for at in range(0, columns, piece):
            value = dot(flipped, right[:, at:at + piece])
            buffers[step % depth, :, at:at + piece] = value.astype(BF16)
        copy(step).start()
    for step in range(max(0, steps - depth), steps):
        copy(step).wait()


def weight_grad(after, left, right, name):
    slots, rows = left.shape
    columns = right.shape[1]
    tile = tile_of(rows, 256 if columns > 2048 else 512)
    return pl.pallas_call(
        weight_grad_body,
        out_shape=[pltpu.HBM((rows, columns), BF16), jax.ShapeDtypeStruct((8, LANES), F32)],
        in_specs=[ANYWHERE] + [IN_VMEM] * 2,
        out_specs=[ANYWHERE, IN_VMEM],
        scratch_shapes=[pltpu.VMEM((4, tile, columns), BF16), pltpu.SemaphoreType.DMA((4,))],
        compiler_params=params(12, slots),
        cost_estimate=cost(0, 2 * LANES),
        name=name,
    )(after, left, right)


def three_parts(value):
    high = value.astype(BF16)
    rest = value - high.astype(F32)
    mid = rest.astype(BF16)
    return high, mid, (rest - mid.astype(F32)).astype(BF16)


def write_chunks(n, total, got, router, outs):
    half = total.shape[1]
    for s in range(n):
        span = slice(s * CAP, (s + 1) * CAP)
        outs[s][:, 0:half] = (total[span, :] + got[span, :].astype(F32)).astype(BF16)
        if router is not None:
            high, mid, low = three_parts(router[span, :])
            lane = lax.broadcasted_iota(jnp.int32, (CAP, LANES), 1)
            outs[s][:, half:] = jnp.where(
                lane == 0, high, jnp.where(lane == 1, mid, jnp.where(lane == 2, low, jnp.zeros_like(low)))
            )


def merge_body(n, after, keep, got, *refs):
    write_chunks(n, keep[...], got, refs[0] if len(refs) > n else None, refs[-n:])


def merge(after, n, keep, got, *router):
    wide = keep.shape[1] + LANES * len(router)
    return pl.pallas_call(
        functools.partial(merge_body, n),
        out_shape=[jax.ShapeDtypeStruct((CAP, wide), BF16)] * n,
        in_specs=[ANYWHERE] + [IN_VMEM] * (2 + len(router)),
        out_specs=[IN_VMEM] * n,
        compiler_params=params(),
        cost_estimate=cost(0, 8 * keep.size),
        name="merge",
    )(after, keep, got, *router)


def combine_body(n, after, weights, *refs):
    chunks, out = refs[:n], refs[-1]
    total = dot(weights[0:CAP, :], chunks[0][...], 0, 0)
    for s in range(1, n):
        total += dot(weights[s * CAP:(s + 1) * CAP, :], chunks[s][...], 0, 0)
    out[...] = total.astype(BF16)


def combine(after, n, weights, chunks):
    half = chunks[0].shape[1]
    return pl.pallas_call(
        functools.partial(combine_body, n),
        out_shape=jax.ShapeDtypeStruct((weights.shape[1], half), BF16),
        in_specs=[ANYWHERE] + [IN_VMEM] * (n + 1),
        out_specs=IN_VMEM,
        compiler_params=params(),
        cost_estimate=cost(2 * weights.size * half, 2 * n * CAP * half),
        name="combine",
    )(after, weights, *chunks)


def combine_router_body(n, half, after, first, second, *refs):
    chunks, out = refs[:n], refs[-1]
    rows = first.shape[1]
    total = jnp.zeros((rows, half), F32)
    score0 = jnp.zeros((rows, LANES), F32)
    score1 = jnp.zeros((rows, LANES), F32)
    for s in range(n):
        span = pl.ds(s * CAP, CAP)
        placed0, placed1 = first[span, :], second[span, :]
        total += dot(placed0 + placed1, chunks[s][:, 0:half], 0, 0)
        score0 += dot(placed0, chunks[s][:, half:], 0, 0)
        score1 += dot(placed1, chunks[s][:, half:], 0, 0)
    out[:, 0:half] = total.astype(BF16)
    out[:, half:] = spread_scores(
        jnp.sum(score0, axis=1, keepdims=True), jnp.sum(score1, axis=1, keepdims=True)
    )


def combine_router(after, n, first, second, chunks):
    wide = chunks[0].shape[1]
    rows = first.shape[1]
    return pl.pallas_call(
        functools.partial(combine_router_body, n, wide - LANES),
        out_shape=jax.ShapeDtypeStruct((rows, wide), BF16),
        in_specs=[ANYWHERE] + [IN_VMEM] * (n + 2),
        out_specs=IN_VMEM,
        compiler_params=params(),
        cost_estimate=cost(2 * first.size * wide, 2 * n * CAP * wide),
        name="combine_router",
    )(after, first, second, *chunks)


def spread_scores(score0, score1):
    rows = score0.shape[0]
    lane = lax.broadcasted_iota(jnp.int32, (rows, LANES), 1)
    out = jnp.zeros((rows, LANES), F32)
    for k, score in enumerate((score0, score1)):
        for p, part in enumerate(three_parts(score)):
            out = jnp.where(lane == 3 * k + p, part.astype(F32), out)
    return out.astype(BF16)


def joined_scores(packed):
    values = packed.astype(F32)
    score0 = values[:, 0:1] + values[:, 1:2] + values[:, 2:3]
    score1 = values[:, 3:4] + values[:, 4:5] + values[:, 5:6]
    return score0, score1


def add_body(after, *refs):
    total = refs[0][...].astype(F32)
    for piece in refs[1:-1]:
        total += piece[...].astype(F32)
    refs[-1][...] = total.astype(BF16)


def add_pieces(after, pieces):
    return pl.pallas_call(
        add_body,
        out_shape=jax.ShapeDtypeStruct(pieces[0].shape, BF16),
        in_specs=[ANYWHERE] + [IN_VMEM] * len(pieces),
        out_specs=IN_VMEM,
        compiler_params=params(),
        cost_estimate=cost(0, 6 * pieces[0].size),
        name="add_pieces",
    )(after, *pieces)


def finish_body(half, count, layer_own, layer_other, *refs):
    own, other = refs[:count], refs[count:2 * count]
    layer, total, score = refs[2 * count:]
    rows = layer.shape[0]
    layer[:, pl.ds(own_half(half), half)] = layer_own[...]
    layer[:, pl.ds(other_half(half), half)] = layer_other[...]
    for pieces, start in ((own, own_half(half)), (other, other_half(half))):
        value = pieces[0][:, 0:half].astype(F32)
        for piece in pieces[1:]:
            value += piece[:, 0:half].astype(F32)
        total[:, pl.ds(start, half)] = value.astype(BF16)
    scores = [[joined_scores(piece[:, half:]) for piece in pieces] for pieces in (own, other)]
    sums = [[sum(part[k] for part in parts) for k in range(2)] for parts in scores]
    lane = lax.broadcasted_iota(jnp.int32, (rows, LANES), 1)
    score[...] = jnp.where(lane == 0, sums[0][0] + sums[1][0], sums[0][1] + sums[1][1]).T[0:2, :]


def finish(half, layer_own, layer_other, own, other):
    rows = own[0].shape[0]
    return pl.pallas_call(
        functools.partial(finish_body, half, len(own)),
        out_shape=[jax.ShapeDtypeStruct((rows, 2 * half), BF16)] * 2
        + [jax.ShapeDtypeStruct((2, rows), F32)],
        in_specs=[IN_VMEM] * (2 + 2 * len(own)),
        out_specs=[IN_VMEM] * 3,
        compiler_params=params(),
        cost_estimate=cost(0, 8 * rows * half),
        name="finish",
    )(layer_own, layer_other, *own, *other)


def from_chips(value):
    count = lax.axis_size("dp")
    if count == 2:
        return [value, shift(value, "dp", 1)]
    gathered = lax.all_gather(value, "dp", axis=0, tiled=False)
    return [gathered[j] for j in range(count)]


def on_device(tokens, expert_ids, gates, out_grad, gate_weight, up_weight, down_weight):
    ids, gates, tokens, out_grad, gate_weight, up_weight, down_weight = (
        pltpu.with_memory_space_constraint(v, pltpu.HBM)
        for v in (expert_ids.T, gates.T, tokens, out_grad, gate_weight, up_weight, down_weight)
    )
    n = lax.axis_size("ed")
    slots = n * CAP
    half = tokens.shape[1] // 2
    hid = gate_weight.shape[1]

    (own_tok, own_grad, own_coef), sent, placing = pick(n, hid, ids, gates, tokens, out_grad)
    arrived = [shift(sent[s - 1], "ed", s) for s in range(1, n)]
    gate_held, gate_done = load(own_coef, gate_weight)
    up_held, up_done = load(gate_done, up_weight)
    direct = stack(up_done, arrived)
    other = shift(direct, "tp", 1)
    rows, hidden, act, slope = forward(n, own_tok, direct, other, gate_held, up_held)
    scaled, gate_pre, up_pre, router, out_part, out_keep = middle(
        n, own_grad, own_coef, direct, other, hidden, act, slope, down_weight
    )
    out_got = shift(out_part, "tp", 1)
    in_part = input_part(False, BF16, slots, gate_pre, up_pre, gate_held, up_held)
    in_got = shift(in_part, "tp", 1)
    out_chunks = merge(router, n, out_keep, out_got)
    out_back = [out_chunks[0]] + [shift(out_chunks[s], "ed", -s) for s in range(1, n)]
    in_keep = input_part(True, F32, slots, gate_pre, up_pre, gate_held, up_held)
    in_chunks = merge(out_back[1], n, in_keep, in_got, router)
    in_back = [in_chunks[0]] + [shift(in_chunks[s], "ed", -s) for s in range(1, n)]
    first, second, weighted = placing
    up_w_grad, done = weight_grad(in_chunks[0], rows, up_pre, "up_grad")
    in_mine = combine_router(done, n, first, second, in_back)
    gate_w_grad, done = weight_grad(in_mine, rows, gate_pre, "gate_grad")
    out_mine = combine(done, n, weighted, out_back)
    down_grad, done = weight_grad(out_mine, hidden, scaled, "down_grad")
    in_own = from_chips(in_mine)
    out_half = add_pieces(done, from_chips(out_mine))
    layer_out, token_grad, gate_grad = finish(
        half, out_half, shift(out_half, "tp", 1),
        in_own, [shift(piece, "tp", 1) for piece in in_own],
    )
    return layer_out, token_grad, gate_grad.T, gate_w_grad, up_w_grad, down_grad


def solution(mesh):
    token_spec = P(("groups", "ed"), None)
    in_specs = (
        token_spec,
        token_spec,
        token_spec,
        token_spec,
        P(None, ("ed", "dp", "tp")),
        P(None, ("ed", "dp", "tp")),
        P(("ed", "dp", "tp"), None),
    )
    out_specs = (
        token_spec,
        token_spec,
        token_spec,
        P("groups", ("ed", "dp", "tp")),
        P("groups", ("ed", "dp", "tp")),
        P(("groups", "ed", "dp", "tp"), None),
    )
    return jax.shard_map(
        on_device, mesh=mesh, in_specs=in_specs, out_specs=out_specs, check_vma=False
    )
```

```python
import functools

import jax
import jax.numpy as jnp
from jax import lax
from jax.experimental import pallas as pl
from jax.experimental.pallas import tpu as pltpu
from jax.sharding import PartitionSpec as P

FF = 7168
CAP = 48
LANES = 128
F32 = jnp.float32
BF16 = jnp.bfloat16


def dot(left, right, left_dim=1, right_dim=0):
    return lax.dot_general(
        left, right, (((left_dim,), (right_dim,)), ((), ())), preferred_element_type=F32
    )


def params(megabytes=6, slots=0):
    scale = 1 if slots <= 256 else 4
    return pltpu.CompilerParams(vmem_limit_bytes=megabytes * scale * 1024 * 1024)


def tile_of(size, most):
    for tile in (1024, 512, 256):
        if tile <= most and size % tile == 0:
            return tile
    return size


def padded(slots):
    return -(-slots // 256) * 256


IN_VMEM = pl.BlockSpec(memory_space=pltpu.VMEM)
ANYWHERE = pl.BlockSpec(memory_space=pl.ANY)


def own_half(half):
    return pl.multiple_of(lax.axis_index("tp") * half, half)


def other_half(half):
    return pl.multiple_of((1 - lax.axis_index("tp")) * half, half)


def cost(flops, nbytes):
    return pl.CostEstimate(flops=int(flops), bytes_accessed=int(nbytes), transcendentals=0)


def shift(value, axis, step):
    count = lax.axis_size(axis)
    return lax.ppermute(value, axis, [(j, (j + step) % count) for j in range(count)])


def pick_body(n, hid, reps, ids, gates, tokens, grads, *outs):
    own_tok, own_grad, own_coef = outs[0:3]
    first, second, weighted = outs[n + 2:]
    rows, width = tokens.shape
    half = width // 2
    upper = (
        lax.broadcasted_iota(jnp.int32, (rows, rows), 0)
        <= lax.broadcasted_iota(jnp.int32, (rows, rows), 1)
    ).astype(BF16)
    me, rep = lax.axis_index("ed"), lax.axis_index("dp") * 2 + lax.axis_index("tp")
    slot_index = lax.broadcasted_iota(jnp.int32, (CAP, rows), 0).astype(F32)
    gate0, gate1 = gates[0:1, :].astype(F32), gates[1:2, :].astype(F32)
    ids0, ids1 = ids[0:1, :], ids[1:2, :]
    for s in range(n):
        owner = lax.rem(me + s, n)
        expert = ((owner * reps + rep) * hid) // FF
        hit0 = jnp.where(ids0 == expert, 1.0, 0.0)
        hit1 = jnp.where(ids1 == expert, 1.0, 0.0)
        chosen = jnp.broadcast_to(hit0 + hit1, (8, rows)).astype(BF16)
        place = dot(chosen, upper)[0:1] - 1.0
        here = jnp.where(place == slot_index, 1.0, 0.0)
        placed0, placed1 = here * hit0, here * hit1
        placed = (placed0 + placed1).astype(BF16)
        weight = placed0 * gate0 + placed1 * gate1
        span = pl.ds(s * CAP, CAP)
        first[span, :] = placed0.astype(BF16)
        second[span, :] = placed1.astype(BF16)
        weighted[span, :] = weight.astype(BF16)
        coef = jnp.broadcast_to(jnp.sum(weight, axis=1, keepdims=True), (CAP, LANES)).astype(BF16)
        if s == 0:
            own_tok[...] = dot(placed, tokens[...]).astype(BF16)
            own_grad[...] = dot(placed, grads[...]).astype(BF16)
            own_coef[...] = coef
        else:
            mine = pl.ds(own_half(half), half)
            out = outs[2 + s]
            out[:, 0:half] = dot(placed, tokens[:, mine]).astype(BF16)
            out[:, half:width] = dot(placed, grads[:, mine]).astype(BF16)
            out[:, width:] = coef


def pick(n, hid, ids, gates, tokens, grads):
    rows, width = tokens.shape
    slots = n * CAP
    out = (
        [jax.ShapeDtypeStruct((CAP, width), BF16)] * 2
        + [jax.ShapeDtypeStruct((CAP, LANES), BF16)]
        + [jax.ShapeDtypeStruct((CAP, width + LANES), BF16)] * (n - 1)
        + [jax.ShapeDtypeStruct((slots, rows), BF16)] * 3
    )
    got = pl.pallas_call(
        functools.partial(pick_body, n, hid, lax.axis_size(("dp", "tp"))),
        out_shape=out,
        compiler_params=params(),
        cost_estimate=cost(4 * slots * rows * width, 8 * rows * width),
        name="pick",
    )(ids, gates, tokens, grads)
    return got[0:3], got[3:n + 2], got[n + 2:]


def load_body(after, weight, held, done, sems):
    rows = weight.shape[0] // sems.shape[0]
    copies = [
        pltpu.make_async_copy(weight.at[pl.ds(j * rows, rows)], held.at[pl.ds(j * rows, rows)], sems.at[j])
        for j in range(sems.shape[0])
    ]
    for copy in copies:
        copy.start()
    done[...] = jnp.zeros_like(done)
    for copy in copies:
        copy.wait()


def load(after, weight):
    return pl.pallas_call(
        load_body,
        out_shape=[pltpu.VMEM(weight.shape, BF16), jax.ShapeDtypeStruct((8, LANES), F32)],
        in_specs=[ANYWHERE] * 2,
        out_specs=[IN_VMEM] * 2,
        scratch_shapes=[pltpu.SemaphoreType.DMA((4,))],
        compiler_params=params(19),
        cost_estimate=cost(0, 2 * LANES),
        name="load",
    )(after, weight)


def stack_body(after, *refs):
    pieces, out = refs[:-1], refs[-1]
    for s, piece in enumerate(pieces):
        out[s * CAP:(s + 1) * CAP, :] = piece[...]


def stack(after, pieces):
    wide = pieces[0].shape[1]
    return pl.pallas_call(
        stack_body,
        out_shape=jax.ShapeDtypeStruct((len(pieces) * CAP, wide), BF16),
        in_specs=[ANYWHERE] + [IN_VMEM] * len(pieces),
        out_specs=IN_VMEM,
        compiler_params=params(),
        cost_estimate=cost(0, 4 * len(pieces) * CAP * wide),
        name="stack",
    )(after, *pieces)


def gather_rows(half, at, own, direct, other, held):
    held[0:CAP, :] = own[...]
    held[CAP:held.shape[0], pl.ds(own_half(half), half)] = direct[:, at:at + half]
    held[CAP:held.shape[0], pl.ds(other_half(half), half)] = other[:, at:at + half]


def clear_padding(slots, ref):
    if ref.shape[0] > slots:
        ref[slots:, :] = jnp.zeros((ref.shape[0] - slots, ref.shape[1]), ref.dtype)


def forward_body(slots, own, direct, other, gate_w, up_w, rows_out, hidden, act, slope):
    width, hid = gate_w.shape
    gather_rows(width // 2, 0, own, direct, other, rows_out.at[pl.ds(0, slots)])
    clear_padding(slots, rows_out)
    for ref in (hidden, act, slope):
        clear_padding(slots, ref)
    rows = rows_out[0:slots, :]
    tile = tile_of(hid, 512)
    for at in range(0, hid, tile):
        span = slice(at, at + tile)
        pre_gate = dot(rows, gate_w[:, span])
        pre_up = dot(rows, up_w[:, span])
        logistic = jax.nn.sigmoid(pre_gate)
        silu = pre_gate * logistic
        hidden[0:slots, span] = (silu * pre_up).astype(BF16)
        act[0:slots, span] = silu.astype(BF16)
        slope[0:slots, span] = (pre_up * logistic * (1.0 + pre_gate * (1.0 - logistic))).astype(BF16)


def forward(n, own, direct, other, gate_w, up_w):
    width, hid = gate_w.shape
    slots = n * CAP
    return pl.pallas_call(
        functools.partial(forward_body, slots),
        out_shape=[
            pltpu.VMEM((padded(slots), width), BF16),
            pltpu.VMEM((padded(slots), hid), BF16),
            pltpu.VMEM((padded(slots), hid), BF16),
            pltpu.VMEM((padded(slots), hid), BF16),
        ],
        in_specs=[IN_VMEM] * 5,
        out_specs=[IN_VMEM] * 4,
        compiler_params=params(6, slots),
        cost_estimate=cost(0, 2 * slots * width),
        name="forward",
    )(own, direct, other, gate_w, up_w)


def streamed(down, buffers, sems, tile, columns):
    def copy(step):
        return pltpu.make_async_copy(
            down.at[pl.ds(step * tile, tile), columns],
            buffers.at[step % buffers.shape[0]],
            sems.at[step % buffers.shape[0]],
        )

    return copy


def middle_body(own, coef_own, direct, other, hidden, act, slope, down, scaled, gate_grad,
                up_grad, router, send, keep, held, total, coef, buffers, sems):
    hid, width = down.shape
    half = width // 2
    slots = held.shape[0]
    depth, tile = buffers.shape[0:2]
    steps = hid // tile
    copy = streamed(down, buffers, sems, tile, slice(None))
    for step in range(min(depth, steps)):
        copy(step).start()
    gather_rows(half, half, own, direct, other, held)
    coef[0:CAP, :] = coef_own[...].astype(F32)
    coef[CAP:, :] = direct[:, width:].astype(F32)
    scale = coef[:, 0:1]
    clear_padding(slots, scaled)
    for ref in (gate_grad, up_grad):
        clear_padding(slots, ref)
    scaled[0:slots, :] = (scale * held[...].astype(F32)).astype(BF16)
    score = jnp.zeros((slots, LANES), F32)
    for step in range(steps):
        span = slice(step * tile, (step + 1) * tile)
        copy(step).wait()
        weight = buffers[step % depth]
        rows = hidden[0:slots, span]
        back = dot(held[...], weight, 1, 1)
        for at in range(0, width, half):
            part = dot(rows, buffers[step % depth, :, at:at + half])
            if step:
                total[:, at:at + half] += part
            else:
                total[:, at:at + half] = part
        if step + depth < steps:
            copy(step + depth).start()
        product = rows.astype(F32) * back
        for lane in range(0, tile // LANES * LANES, LANES):
            score += product[:, lane:lane + LANES]
        if tile % LANES:
            rest = jnp.sum(product[:, tile // LANES * LANES:], axis=1, keepdims=True)
            score += jnp.where(lax.broadcasted_iota(jnp.int32, score.shape, 1) == 0, rest, 0.0)
        grad = scale * back
        gate_grad[0:slots, span] = (grad * slope[0:slots, span].astype(F32)).astype(BF16)
        up_grad[0:slots, span] = (grad * act[0:slots, span].astype(F32)).astype(BF16)
    send[...] = total[:, pl.ds(other_half(half), half)].astype(BF16)
    keep[...] = total[:, pl.ds(own_half(half), half)]
    router[...] = jnp.broadcast_to(jnp.sum(score, axis=1, keepdims=True), router.shape)


def middle(n, own, coef_own, direct, other, hidden, act, slope, down):
    hid, width = down.shape
    half = width // 2
    slots = n * CAP
    tile = tile_of(hid, 256)
    return pl.pallas_call(
        middle_body,
        out_shape=[
            pltpu.VMEM((padded(slots), width), BF16),
            pltpu.VMEM((padded(slots), hid), BF16),
            pltpu.VMEM((padded(slots), hid), BF16),
            jax.ShapeDtypeStruct((slots, LANES), F32),
            jax.ShapeDtypeStruct((slots, half), BF16),
            jax.ShapeDtypeStruct((slots, half), F32),
        ],
        in_specs=[IN_VMEM] * 7 + [ANYWHERE],
        out_specs=[IN_VMEM] * 6,
        scratch_shapes=[
            pltpu.VMEM((slots, width), BF16),
            pltpu.VMEM((slots, width), F32),
            pltpu.VMEM((slots, LANES), F32),
            pltpu.VMEM((4, tile, width), BF16),
            pltpu.SemaphoreType.DMA((4,)),
        ],
        input_output_aliases={5: 2, 6: 1},
        compiler_params=params(9, slots),
        cost_estimate=cost(4 * slots * width * hid, 2 * width * hid),
        name="middle",
    )(own, coef_own, direct, other, hidden, act, slope, down)


def input_body(mine, gate_grad, up_grad, gate_w, up_w, out):
    slots, half = out.shape
    start = own_half(half) if mine else other_half(half)
    tile = tile_of(half, 256)
    for at in range(0, half, tile):
        span = pl.ds(start + at, tile)
        value = dot(gate_grad[0:slots, :], gate_w[span, :], 1, 1)
        value += dot(up_grad[0:slots, :], up_w[span, :], 1, 1)
        out[:, at:at + tile] = value.astype(out.dtype)


def input_part(mine, kind, slots, gate_grad, up_grad, gate_w, up_w):
    width, hid = gate_w.shape
    return pl.pallas_call(
        functools.partial(input_body, mine),
        out_shape=jax.ShapeDtypeStruct((slots, width // 2), kind),
        in_specs=[IN_VMEM] * 4,
        out_specs=IN_VMEM,
        compiler_params=params(6, slots),
        cost_estimate=cost(2 * slots * width * hid, 2 * slots * width),
        name="input_keep" if mine else "input_send",
    )(gate_grad, up_grad, gate_w, up_w)


def weight_grad_body(after, left, right, out, done, buffers, sems):
    done[...] = jnp.zeros_like(done)
    depth, tile, columns = buffers.shape
    steps = out.shape[0] // tile
    piece = tile_of(columns, 512)

    def copy(step):
        slot = step % depth
        return pltpu.make_async_copy(
            buffers.at[slot], out.at[pl.ds(step * tile, tile), :], sems.at[slot]
        )

    for step in range(steps):
        flipped = left[:, step * tile:(step + 1) * tile].T
        if step >= depth:
            copy(step - depth).wait()
        for at in range(0, columns, piece):
            value = dot(flipped, right[:, at:at + piece])
            buffers[step % depth, :, at:at + piece] = value.astype(BF16)
        copy(step).start()
    for step in range(max(0, steps - depth), steps):
        copy(step).wait()


def weight_grad(after, left, right, name):
    slots, rows = left.shape
    columns = right.shape[1]
    tile = tile_of(rows, 256 if columns > 2048 else 512)
    return pl.pallas_call(
        weight_grad_body,
        out_shape=[pltpu.HBM((rows, columns), BF16), jax.ShapeDtypeStruct((8, LANES), F32)],
        in_specs=[ANYWHERE] + [IN_VMEM] * 2,
        out_specs=[ANYWHERE, IN_VMEM],
        scratch_shapes=[pltpu.VMEM((4, tile, columns), BF16), pltpu.SemaphoreType.DMA((4,))],
        compiler_params=params(12, slots),
        cost_estimate=cost(0, 2 * LANES),
        name=name,
    )(after, left, right)


def three_parts(value):
    high = value.astype(BF16)
    rest = value - high.astype(F32)
    mid = rest.astype(BF16)
    return high, mid, (rest - mid.astype(F32)).astype(BF16)


def write_chunks(chosen, total, got, router, outs):
    half = total.shape[1]
    for j, s in enumerate(chosen):
        span = slice(s * CAP, (s + 1) * CAP)
        outs[j][:, 0:half] = (total[span, :] + got[span, :].astype(F32)).astype(BF16)
        if router is not None:
            high, mid, low = three_parts(router[span, :])
            lane = lax.broadcasted_iota(jnp.int32, (CAP, LANES), 1)
            outs[j][:, half:] = jnp.where(
                lane == 0, high, jnp.where(lane == 1, mid, jnp.where(lane == 2, low, jnp.zeros_like(low)))
            )


def merge_body(chosen, after, keep, got, *refs):
    count = len(chosen)
    write_chunks(chosen, keep, got, refs[0] if len(refs) > count else None, refs[-count:])


def merge(after, chosen, keep, got, *router):
    wide = keep.shape[1] + LANES * len(router)
    return pl.pallas_call(
        functools.partial(merge_body, chosen),
        out_shape=[jax.ShapeDtypeStruct((CAP, wide), BF16)] * len(chosen),
        in_specs=[ANYWHERE] + [IN_VMEM] * (2 + len(router)),
        out_specs=[IN_VMEM] * len(chosen),
        compiler_params=params(),
        cost_estimate=cost(0, 8 * keep.size),
        name="merge",
    )(after, keep, got, *router)


def combine_body(n, after, weights, *refs):
    chunks, out = refs[:n], refs[-1]
    total = dot(weights[0:CAP, :], chunks[0][...], 0, 0)
    for s in range(1, n):
        total += dot(weights[s * CAP:(s + 1) * CAP, :], chunks[s][...], 0, 0)
    out[...] = total.astype(BF16)


def combine(after, n, weights, chunks):
    half = chunks[0].shape[1]
    return pl.pallas_call(
        functools.partial(combine_body, n),
        out_shape=jax.ShapeDtypeStruct((weights.shape[1], half), BF16),
        in_specs=[ANYWHERE] + [IN_VMEM] * (n + 1),
        out_specs=IN_VMEM,
        compiler_params=params(),
        cost_estimate=cost(2 * weights.size * half, 2 * n * CAP * half),
        name="combine",
    )(after, weights, *chunks)


def combine_router_body(n, half, after, first, second, *refs):
    chunks, out = refs[:n], refs[-1]
    rows = first.shape[1]
    total = jnp.zeros((rows, half), F32)
    score0 = jnp.zeros((rows, LANES), F32)
    score1 = jnp.zeros((rows, LANES), F32)
    for s in range(n):
        span = pl.ds(s * CAP, CAP)
        placed0, placed1 = first[span, :], second[span, :]
        total += dot(placed0 + placed1, chunks[s][:, 0:half], 0, 0)
        score0 += dot(placed0, chunks[s][:, half:], 0, 0)
        score1 += dot(placed1, chunks[s][:, half:], 0, 0)
    out[:, 0:half] = total.astype(BF16)
    out[:, half:] = spread_scores(
        jnp.sum(score0, axis=1, keepdims=True), jnp.sum(score1, axis=1, keepdims=True)
    )


def combine_router(after, n, first, second, chunks):
    wide = chunks[0].shape[1]
    rows = first.shape[1]
    return pl.pallas_call(
        functools.partial(combine_router_body, n, wide - LANES),
        out_shape=jax.ShapeDtypeStruct((rows, wide), BF16),
        in_specs=[ANYWHERE] + [IN_VMEM] * (n + 2),
        out_specs=IN_VMEM,
        compiler_params=params(),
        cost_estimate=cost(2 * first.size * wide, 2 * n * CAP * wide),
        name="combine_router",
    )(after, first, second, *chunks)


def spread_scores(score0, score1):
    rows = score0.shape[0]
    lane = lax.broadcasted_iota(jnp.int32, (rows, LANES), 1)
    out = jnp.zeros((rows, LANES), F32)
    for k, score in enumerate((score0, score1)):
        for p, part in enumerate(three_parts(score)):
            out = jnp.where(lane == 3 * k + p, part.astype(F32), out)
    return out.astype(BF16)


def joined_scores(packed):
    values = packed.astype(F32)
    score0 = values[:, 0:1] + values[:, 1:2] + values[:, 2:3]
    score1 = values[:, 3:4] + values[:, 4:5] + values[:, 5:6]
    return score0, score1


def add_body(after, *refs):
    total = refs[0][...].astype(F32)
    for piece in refs[1:-1]:
        total += piece[...].astype(F32)
    refs[-1][...] = total.astype(BF16)


def add_pieces(after, pieces):
    return pl.pallas_call(
        add_body,
        out_shape=jax.ShapeDtypeStruct(pieces[0].shape, BF16),
        in_specs=[ANYWHERE] + [IN_VMEM] * len(pieces),
        out_specs=IN_VMEM,
        compiler_params=params(),
        cost_estimate=cost(0, 6 * pieces[0].size),
        name="add_pieces",
    )(after, *pieces)


def finish_body(half, count, layer_own, layer_other, *refs):
    own, other = refs[:count], refs[count:2 * count]
    layer, total, score = refs[2 * count:]
    rows = layer.shape[0]
    layer[:, pl.ds(own_half(half), half)] = layer_own[...]
    layer[:, pl.ds(other_half(half), half)] = layer_other[...]
    for pieces, start in ((own, own_half(half)), (other, other_half(half))):
        value = pieces[0][:, 0:half].astype(F32)
        for piece in pieces[1:]:
            value += piece[:, 0:half].astype(F32)
        total[:, pl.ds(start, half)] = value.astype(BF16)
    scores = [[joined_scores(piece[:, half:]) for piece in pieces] for pieces in (own, other)]
    sums = [[sum(part[k] for part in parts) for k in range(2)] for parts in scores]
    lane = lax.broadcasted_iota(jnp.int32, (rows, LANES), 1)
    score[...] = jnp.where(lane == 0, sums[0][0] + sums[1][0], sums[0][1] + sums[1][1]).T[0:2, :]


def finish(half, layer_own, layer_other, own, other):
    rows = own[0].shape[0]
    return pl.pallas_call(
        functools.partial(finish_body, half, len(own)),
        out_shape=[jax.ShapeDtypeStruct((rows, 2 * half), BF16)] * 2
        + [jax.ShapeDtypeStruct((2, rows), F32)],
        in_specs=[IN_VMEM] * (2 + 2 * len(own)),
        out_specs=[IN_VMEM] * 3,
        compiler_params=params(),
        cost_estimate=cost(0, 8 * rows * half),
        name="finish",
    )(layer_own, layer_other, *own, *other)


def from_chips(value):
    count = lax.axis_size("dp")
    if count == 2:
        return [value, shift(value, "dp", 1)]
    gathered = lax.all_gather(value, "dp", axis=0, tiled=False)
    return [gathered[j] for j in range(count)]


def on_device(tokens, expert_ids, gates, out_grad, gate_weight, up_weight, down_weight):
    ids, gates, tokens, out_grad, gate_weight, up_weight, down_weight = (
        pltpu.with_memory_space_constraint(v, pltpu.HBM)
        for v in (expert_ids.T, gates.T, tokens, out_grad, gate_weight, up_weight, down_weight)
    )
    n = lax.axis_size("ed")
    slots = n * CAP
    half = tokens.shape[1] // 2
    hid = gate_weight.shape[1]

    (own_tok, own_grad, own_coef), sent, placing = pick(n, hid, ids, gates, tokens, out_grad)
    arrived = [shift(sent[s - 1], "ed", s) for s in range(1, n)]
    gate_held, gate_done = load(own_coef, gate_weight)
    up_held, up_done = load(gate_done, up_weight)
    direct = stack(up_done, arrived)
    other = shift(direct, "tp", 1)
    rows, hidden, act, slope = forward(n, own_tok, direct, other, gate_held, up_held)
    scaled, gate_pre, up_pre, router, out_part, out_keep = middle(
        n, own_grad, own_coef, direct, other, hidden, act, slope, down_weight
    )
    out_got = shift(out_part, "tp", 1)
    in_part = input_part(False, BF16, slots, gate_pre, up_pre, gate_held, up_held)
    in_got = shift(in_part, "tp", 1)
    in_keep = input_part(True, F32, slots, gate_pre, up_pre, gate_held, up_held)
    in_chunks = merge(router, range(n), in_keep, in_got, router)
    in_back = [in_chunks[0]] + [shift(in_chunks[s], "ed", -s) for s in range(1, n)]
    first, second, weighted = placing
    up_w_grad, done = weight_grad(in_chunks[0], rows, up_pre, "up_grad")
    out_chunks = merge(done, range(n), out_keep, out_got)
    out_back = [out_chunks[0]] + [shift(out_chunks[s], "ed", -s) for s in range(1, n)]
    in_mine = combine_router(done, n, first, second, in_back)
    gate_w_grad, done = weight_grad(in_mine, rows, gate_pre, "gate_grad")
    out_mine = combine(done, n, weighted, out_back)
    down_grad, done = weight_grad(out_mine, hidden, scaled, "down_grad")
    in_own = from_chips(in_mine)
    out_half = add_pieces(done, from_chips(out_mine))
    layer_out, token_grad, gate_grad = finish(
        half, out_half, shift(out_half, "tp", 1),
        in_own, [shift(piece, "tp", 1) for piece in in_own],
    )
    return layer_out, token_grad, gate_grad.T, gate_w_grad, up_w_grad, down_grad


def solution(mesh):
    token_spec = P(("groups", "ed"), None)
    in_specs = (
        token_spec,
        token_spec,
        token_spec,
        token_spec,
        P(None, ("ed", "dp", "tp")),
        P(None, ("ed", "dp", "tp")),
        P(("ed", "dp", "tp"), None),
    )
    out_specs = (
        token_spec,
        token_spec,
        token_spec,
        P("groups", ("ed", "dp", "tp")),
        P("groups", ("ed", "dp", "tp")),
        P(("groups", "ed", "dp", "tp"), None),
    )
    return jax.shard_map(
        on_device, mesh=mesh, in_specs=in_specs, out_specs=out_specs, check_vma=False
    )
```

```python
import functools

import jax
import jax.numpy as jnp
from jax import lax
from jax.experimental import pallas as pl
from jax.experimental.pallas import tpu as pltpu
from jax.sharding import PartitionSpec as P

FF = 7168
CAP = 48
LANES = 128
F32 = jnp.float32
BF16 = jnp.bfloat16


def dot(left, right, left_dim=1, right_dim=0):
    return lax.dot_general(
        left, right, (((left_dim,), (right_dim,)), ((), ())), preferred_element_type=F32
    )


def params(megabytes=6, slots=0):
    scale = 1 if slots <= 256 else 4
    return pltpu.CompilerParams(vmem_limit_bytes=megabytes * scale * 1024 * 1024)


def tile_of(size, most):
    for tile in (1024, 512, 256):
        if tile <= most and size % tile == 0:
            return tile
    return size


def padded(slots):
    return -(-slots // 256) * 256


IN_VMEM = pl.BlockSpec(memory_space=pltpu.VMEM)
ANYWHERE = pl.BlockSpec(memory_space=pl.ANY)


def own_half(half):
    return pl.multiple_of(lax.axis_index("tp") * half, half)


def other_half(half):
    return pl.multiple_of((1 - lax.axis_index("tp")) * half, half)


def cost(flops, nbytes):
    return pl.CostEstimate(flops=int(flops), bytes_accessed=int(nbytes), transcendentals=0)


def shift(value, axis, step):
    count = lax.axis_size(axis)
    return lax.ppermute(value, axis, [(j, (j + step) % count) for j in range(count)])


def pick_body(n, hid, reps, ids, gates, tokens, grads, *outs):
    own_tok, own_grad, own_coef = outs[0:3]
    first, second, weighted = outs[n + 2:]
    rows, width = tokens.shape
    half = width // 2
    upper = (
        lax.broadcasted_iota(jnp.int32, (rows, rows), 0)
        <= lax.broadcasted_iota(jnp.int32, (rows, rows), 1)
    ).astype(BF16)
    me, rep = lax.axis_index("ed"), lax.axis_index("dp") * 2 + lax.axis_index("tp")
    slot_index = lax.broadcasted_iota(jnp.int32, (CAP, rows), 0).astype(F32)
    gate0, gate1 = gates[0:1, :].astype(F32), gates[1:2, :].astype(F32)
    ids0, ids1 = ids[0:1, :], ids[1:2, :]
    for s in range(n):
        owner = lax.rem(me + s, n)
        expert = ((owner * reps + rep) * hid) // FF
        hit0 = jnp.where(ids0 == expert, 1.0, 0.0)
        hit1 = jnp.where(ids1 == expert, 1.0, 0.0)
        chosen = jnp.broadcast_to(hit0 + hit1, (8, rows)).astype(BF16)
        place = dot(chosen, upper)[0:1] - 1.0
        here = jnp.where(place == slot_index, 1.0, 0.0)
        placed0, placed1 = here * hit0, here * hit1
        placed = (placed0 + placed1).astype(BF16)
        weight = placed0 * gate0 + placed1 * gate1
        span = pl.ds(s * CAP, CAP)
        first[span, :] = placed0.astype(BF16)
        second[span, :] = placed1.astype(BF16)
        weighted[span, :] = weight.astype(BF16)
        coef = jnp.broadcast_to(jnp.sum(weight, axis=1, keepdims=True), (CAP, LANES)).astype(BF16)
        if s == 0:
            own_tok[...] = dot(placed, tokens[...]).astype(BF16)
            own_grad[...] = dot(placed, grads[...]).astype(BF16)
            own_coef[...] = coef
        else:
            mine = pl.ds(own_half(half), half)
            out = outs[2 + s]
            out[:, 0:half] = dot(placed, tokens[:, mine]).astype(BF16)
            out[:, half:width] = dot(placed, grads[:, mine]).astype(BF16)
            out[:, width:] = coef


def pick(n, hid, ids, gates, tokens, grads):
    rows, width = tokens.shape
    slots = n * CAP
    out = (
        [jax.ShapeDtypeStruct((CAP, width), BF16)] * 2
        + [jax.ShapeDtypeStruct((CAP, LANES), BF16)]
        + [jax.ShapeDtypeStruct((CAP, width + LANES), BF16)] * (n - 1)
        + [jax.ShapeDtypeStruct((slots, rows), BF16)] * 3
    )
    got = pl.pallas_call(
        functools.partial(pick_body, n, hid, lax.axis_size(("dp", "tp"))),
        out_shape=out,
        compiler_params=params(),
        cost_estimate=cost(4 * slots * rows * width, 8 * rows * width),
        name="pick",
    )(ids, gates, tokens, grads)
    return got[0:3], got[3:n + 2], got[n + 2:]


def load_body(after, weight, held, done, sems):
    rows = weight.shape[0] // sems.shape[0]
    copies = [
        pltpu.make_async_copy(weight.at[pl.ds(j * rows, rows)], held.at[pl.ds(j * rows, rows)], sems.at[j])
        for j in range(sems.shape[0])
    ]
    for copy in copies:
        copy.start()
    done[...] = jnp.zeros_like(done)
    for copy in copies:
        copy.wait()


def load(after, weight):
    return pl.pallas_call(
        load_body,
        out_shape=[pltpu.VMEM(weight.shape, BF16), jax.ShapeDtypeStruct((8, LANES), F32)],
        in_specs=[ANYWHERE] * 2,
        out_specs=[IN_VMEM] * 2,
        scratch_shapes=[pltpu.SemaphoreType.DMA((4,))],
        compiler_params=params(19),
        cost_estimate=cost(0, 2 * LANES),
        name="load",
    )(after, weight)


def stack_body(after, *refs):
    pieces, out = refs[:-1], refs[-1]
    for s, piece in enumerate(pieces):
        out[s * CAP:(s + 1) * CAP, :] = piece[...]


def stack(after, pieces):
    wide = pieces[0].shape[1]
    return pl.pallas_call(
        stack_body,
        out_shape=jax.ShapeDtypeStruct((len(pieces) * CAP, wide), BF16),
        in_specs=[ANYWHERE] + [IN_VMEM] * len(pieces),
        out_specs=IN_VMEM,
        compiler_params=params(),
        cost_estimate=cost(0, 4 * len(pieces) * CAP * wide),
        name="stack",
    )(after, *pieces)


def gather_rows(half, at, own, direct, other, held):
    held[0:CAP, :] = own[...]
    held[CAP:held.shape[0], pl.ds(own_half(half), half)] = direct[:, at:at + half]
    held[CAP:held.shape[0], pl.ds(other_half(half), half)] = other[:, at:at + half]


def clear_padding(slots, ref):
    if ref.shape[0] > slots:
        ref[slots:, :] = jnp.zeros((ref.shape[0] - slots, ref.shape[1]), ref.dtype)


def forward_body(slots, own, direct, other, gate_w, up_w, rows_out, hidden, act, slope):
    width, hid = gate_w.shape
    gather_rows(width // 2, 0, own, direct, other, rows_out.at[pl.ds(0, slots)])
    clear_padding(slots, rows_out)
    for ref in (hidden, act, slope):
        clear_padding(slots, ref)
    rows = rows_out[0:slots, :]
    tile = tile_of(hid, 512)
    for at in range(0, hid, tile):
        span = slice(at, at + tile)
        pre_gate = dot(rows, gate_w[:, span])
        pre_up = dot(rows, up_w[:, span])
        logistic = jax.nn.sigmoid(pre_gate)
        silu = pre_gate * logistic
        hidden[0:slots, span] = (silu * pre_up).astype(BF16)
        act[0:slots, span] = silu.astype(BF16)
        slope[0:slots, span] = (pre_up * logistic * (1.0 + pre_gate * (1.0 - logistic))).astype(BF16)


def forward(n, own, direct, other, gate_w, up_w):
    width, hid = gate_w.shape
    slots = n * CAP
    return pl.pallas_call(
        functools.partial(forward_body, slots),
        out_shape=[
            pltpu.VMEM((padded(slots), width), BF16),
            pltpu.VMEM((padded(slots), hid), BF16),
            pltpu.VMEM((padded(slots), hid), BF16),
            pltpu.VMEM((padded(slots), hid), BF16),
        ],
        in_specs=[IN_VMEM] * 5,
        out_specs=[IN_VMEM] * 4,
        compiler_params=params(6, slots),
        cost_estimate=cost(0, 2 * slots * width),
        name="forward",
    )(own, direct, other, gate_w, up_w)


def streamed(down, buffers, sems, tile, columns):
    def copy(step):
        return pltpu.make_async_copy(
            down.at[pl.ds(step * tile, tile), columns],
            buffers.at[step % buffers.shape[0]],
            sems.at[step % buffers.shape[0]],
        )

    return copy


def middle_body(own, coef_own, direct, other, hidden, act, slope, down, scaled, gate_grad,
                up_grad, router, send, keep, held, total, coef, buffers, sems):
    hid, width = down.shape
    half = width // 2
    slots = held.shape[0]
    depth, tile = buffers.shape[0:2]
    steps = hid // tile
    copy = streamed(down, buffers, sems, tile, slice(None))
    for step in range(min(depth, steps)):
        copy(step).start()
    gather_rows(half, half, own, direct, other, held)
    coef[0:CAP, :] = coef_own[...].astype(F32)
    coef[CAP:, :] = direct[:, width:].astype(F32)
    scale = coef[:, 0:1]
    clear_padding(slots, scaled)
    for ref in (gate_grad, up_grad):
        clear_padding(slots, ref)
    scaled[0:slots, :] = (scale * held[...].astype(F32)).astype(BF16)
    score = jnp.zeros((slots, LANES), F32)
    for step in range(steps):
        span = slice(step * tile, (step + 1) * tile)
        copy(step).wait()
        weight = buffers[step % depth]
        rows = hidden[0:slots, span]
        back = dot(held[...], weight, 1, 1)
        for at in range(0, width, half):
            part = dot(rows, buffers[step % depth, :, at:at + half])
            if step:
                total[:, at:at + half] += part
            else:
                total[:, at:at + half] = part
        if step + depth < steps:
            copy(step + depth).start()
        product = rows.astype(F32) * back
        for lane in range(0, tile // LANES * LANES, LANES):
            score += product[:, lane:lane + LANES]
        if tile % LANES:
            rest = jnp.sum(product[:, tile // LANES * LANES:], axis=1, keepdims=True)
            score += jnp.where(lax.broadcasted_iota(jnp.int32, score.shape, 1) == 0, rest, 0.0)
        grad = scale * back
        gate_grad[0:slots, span] = (grad * slope[0:slots, span].astype(F32)).astype(BF16)
        up_grad[0:slots, span] = (grad * act[0:slots, span].astype(F32)).astype(BF16)
    send[...] = total[:, pl.ds(other_half(half), half)].astype(BF16)
    keep[...] = total[:, pl.ds(own_half(half), half)]
    router[...] = jnp.broadcast_to(jnp.sum(score, axis=1, keepdims=True), router.shape)


def middle(n, own, coef_own, direct, other, hidden, act, slope, down):
    hid, width = down.shape
    half = width // 2
    slots = n * CAP
    tile = tile_of(hid, 512)
    return pl.pallas_call(
        middle_body,
        out_shape=[
            pltpu.VMEM((padded(slots), width), BF16),
            pltpu.VMEM((padded(slots), hid), BF16),
            pltpu.VMEM((padded(slots), hid), BF16),
            jax.ShapeDtypeStruct((slots, LANES), F32),
            jax.ShapeDtypeStruct((slots, half), BF16),
            jax.ShapeDtypeStruct((slots, half), F32),
        ],
        in_specs=[IN_VMEM] * 7 + [ANYWHERE],
        out_specs=[IN_VMEM] * 6,
        scratch_shapes=[
            pltpu.VMEM((slots, width), BF16),
            pltpu.VMEM((slots, width), F32),
            pltpu.VMEM((slots, LANES), F32),
            pltpu.VMEM((2, tile, width), BF16),
            pltpu.SemaphoreType.DMA((2,)),
        ],
        input_output_aliases={5: 2, 6: 1},
        compiler_params=params(9, slots),
        cost_estimate=cost(4 * slots * width * hid, 2 * width * hid),
        name="middle",
    )(own, coef_own, direct, other, hidden, act, slope, down)


def input_body(mine, gate_grad, up_grad, gate_w, up_w, out):
    slots, half = out.shape
    start = own_half(half) if mine else other_half(half)
    tile = tile_of(half, 256)
    for at in range(0, half, tile):
        span = pl.ds(start + at, tile)
        value = dot(gate_grad[0:slots, :], gate_w[span, :], 1, 1)
        value += dot(up_grad[0:slots, :], up_w[span, :], 1, 1)
        out[:, at:at + tile] = value.astype(out.dtype)


def input_part(mine, kind, slots, gate_grad, up_grad, gate_w, up_w):
    width, hid = gate_w.shape
    return pl.pallas_call(
        functools.partial(input_body, mine),
        out_shape=jax.ShapeDtypeStruct((slots, width // 2), kind),
        in_specs=[IN_VMEM] * 4,
        out_specs=IN_VMEM,
        compiler_params=params(6, slots),
        cost_estimate=cost(2 * slots * width * hid, 2 * slots * width),
        name="input_keep" if mine else "input_send",
    )(gate_grad, up_grad, gate_w, up_w)


def weight_grad_body(after, left, right, out, done, buffers, sems):
    done[...] = jnp.zeros_like(done)
    depth, tile, columns = buffers.shape
    steps = out.shape[0] // tile
    piece = tile_of(columns, 512)

    def copy(step):
        slot = step % depth
        return pltpu.make_async_copy(
            buffers.at[slot], out.at[pl.ds(step * tile, tile), :], sems.at[slot]
        )

    for step in range(steps):
        flipped = left[:, step * tile:(step + 1) * tile].T
        if step >= depth:
            copy(step - depth).wait()
        for at in range(0, columns, piece):
            value = dot(flipped, right[:, at:at + piece])
            buffers[step % depth, :, at:at + piece] = value.astype(BF16)
        copy(step).start()
    for step in range(max(0, steps - depth), steps):
        copy(step).wait()


def weight_grad(after, left, right, name):
    slots, rows = left.shape
    columns = right.shape[1]
    tile = tile_of(rows, 256 if columns > 2048 else 512)
    return pl.pallas_call(
        weight_grad_body,
        out_shape=[pltpu.HBM((rows, columns), BF16), jax.ShapeDtypeStruct((8, LANES), F32)],
        in_specs=[ANYWHERE] + [IN_VMEM] * 2,
        out_specs=[ANYWHERE, IN_VMEM],
        scratch_shapes=[pltpu.VMEM((4, tile, columns), BF16), pltpu.SemaphoreType.DMA((4,))],
        compiler_params=params(12, slots),
        cost_estimate=cost(0, 2 * LANES),
        name=name,
    )(after, left, right)


def three_parts(value):
    high = value.astype(BF16)
    rest = value - high.astype(F32)
    mid = rest.astype(BF16)
    return high, mid, (rest - mid.astype(F32)).astype(BF16)


def write_chunks(chosen, total, got, router, outs):
    half = total.shape[1]
    for j, s in enumerate(chosen):
        span = slice(s * CAP, (s + 1) * CAP)
        outs[j][:, 0:half] = (total[span, :] + got[span, :].astype(F32)).astype(BF16)
        if router is not None:
            high, mid, low = three_parts(router[span, :])
            lane = lax.broadcasted_iota(jnp.int32, (CAP, LANES), 1)
            outs[j][:, half:] = jnp.where(
                lane == 0, high, jnp.where(lane == 1, mid, jnp.where(lane == 2, low, jnp.zeros_like(low)))
            )


def merge_body(chosen, after, keep, got, *refs):
    count = len(chosen)
    write_chunks(chosen, keep, got, refs[0] if len(refs) > count else None, refs[-count:])


def merge(after, chosen, keep, got, *router):
    wide = keep.shape[1] + LANES * len(router)
    return pl.pallas_call(
        functools.partial(merge_body, chosen),
        out_shape=[jax.ShapeDtypeStruct((CAP, wide), BF16)] * len(chosen),
        in_specs=[ANYWHERE] + [IN_VMEM] * (2 + len(router)),
        out_specs=[IN_VMEM] * len(chosen),
        compiler_params=params(),
        cost_estimate=cost(0, 8 * keep.size),
        name="merge",
    )(after, keep, got, *router)


def combine_body(n, after, weights, *refs):
    chunks, out = refs[:n], refs[-1]
    total = dot(weights[0:CAP, :], chunks[0][...], 0, 0)
    for s in range(1, n):
        total += dot(weights[s * CAP:(s + 1) * CAP, :], chunks[s][...], 0, 0)
    out[...] = total.astype(BF16)


def combine(after, n, weights, chunks):
    half = chunks[0].shape[1]
    return pl.pallas_call(
        functools.partial(combine_body, n),
        out_shape=jax.ShapeDtypeStruct((weights.shape[1], half), BF16),
        in_specs=[ANYWHERE] + [IN_VMEM] * (n + 1),
        out_specs=IN_VMEM,
        compiler_params=params(),
        cost_estimate=cost(2 * weights.size * half, 2 * n * CAP * half),
        name="combine",
    )(after, weights, *chunks)


def combine_router_body(n, half, after, first, second, *refs):
    chunks, out = refs[:n], refs[-1]
    rows = first.shape[1]
    total = jnp.zeros((rows, half), F32)
    score0 = jnp.zeros((rows, LANES), F32)
    score1 = jnp.zeros((rows, LANES), F32)
    for s in range(n):
        span = pl.ds(s * CAP, CAP)
        placed0, placed1 = first[span, :], second[span, :]
        total += dot(placed0 + placed1, chunks[s][:, 0:half], 0, 0)
        score0 += dot(placed0, chunks[s][:, half:], 0, 0)
        score1 += dot(placed1, chunks[s][:, half:], 0, 0)
    out[:, 0:half] = total.astype(BF16)
    out[:, half:] = spread_scores(
        jnp.sum(score0, axis=1, keepdims=True), jnp.sum(score1, axis=1, keepdims=True)
    )


def combine_router(after, n, first, second, chunks):
    wide = chunks[0].shape[1]
    rows = first.shape[1]
    return pl.pallas_call(
        functools.partial(combine_router_body, n, wide - LANES),
        out_shape=jax.ShapeDtypeStruct((rows, wide), BF16),
        in_specs=[ANYWHERE] + [IN_VMEM] * (n + 2),
        out_specs=IN_VMEM,
        compiler_params=params(),
        cost_estimate=cost(2 * first.size * wide, 2 * n * CAP * wide),
        name="combine_router",
    )(after, first, second, *chunks)


def spread_scores(score0, score1):
    rows = score0.shape[0]
    lane = lax.broadcasted_iota(jnp.int32, (rows, LANES), 1)
    out = jnp.zeros((rows, LANES), F32)
    for k, score in enumerate((score0, score1)):
        for p, part in enumerate(three_parts(score)):
            out = jnp.where(lane == 3 * k + p, part.astype(F32), out)
    return out.astype(BF16)


def joined_scores(packed):
    values = packed.astype(F32)
    score0 = values[:, 0:1] + values[:, 1:2] + values[:, 2:3]
    score1 = values[:, 3:4] + values[:, 4:5] + values[:, 5:6]
    return score0, score1


def add_body(after, *refs):
    total = refs[0][...].astype(F32)
    for piece in refs[1:-1]:
        total += piece[...].astype(F32)
    refs[-1][...] = total.astype(BF16)


def add_pieces(after, pieces):
    return pl.pallas_call(
        add_body,
        out_shape=jax.ShapeDtypeStruct(pieces[0].shape, BF16),
        in_specs=[ANYWHERE] + [IN_VMEM] * len(pieces),
        out_specs=IN_VMEM,
        compiler_params=params(),
        cost_estimate=cost(0, 6 * pieces[0].size),
        name="add_pieces",
    )(after, *pieces)


def finish_body(half, count, layer_own, layer_other, *refs):
    own, other = refs[:count], refs[count:2 * count]
    layer, total, score = refs[2 * count:]
    rows = layer.shape[0]
    layer[:, pl.ds(own_half(half), half)] = layer_own[...]
    layer[:, pl.ds(other_half(half), half)] = layer_other[...]
    for pieces, start in ((own, own_half(half)), (other, other_half(half))):
        value = pieces[0][:, 0:half].astype(F32)
        for piece in pieces[1:]:
            value += piece[:, 0:half].astype(F32)
        total[:, pl.ds(start, half)] = value.astype(BF16)
    scores = [[joined_scores(piece[:, half:]) for piece in pieces] for pieces in (own, other)]
    sums = [[sum(part[k] for part in parts) for k in range(2)] for parts in scores]
    lane = lax.broadcasted_iota(jnp.int32, (rows, LANES), 1)
    score[...] = jnp.where(lane == 0, sums[0][0] + sums[1][0], sums[0][1] + sums[1][1]).T[0:2, :]


def finish(half, layer_own, layer_other, own, other):
    rows = own[0].shape[0]
    return pl.pallas_call(
        functools.partial(finish_body, half, len(own)),
        out_shape=[jax.ShapeDtypeStruct((rows, 2 * half), BF16)] * 2
        + [jax.ShapeDtypeStruct((2, rows), F32)],
        in_specs=[IN_VMEM] * (2 + 2 * len(own)),
        out_specs=[IN_VMEM] * 3,
        compiler_params=params(),
        cost_estimate=cost(0, 8 * rows * half),
        name="finish",
    )(layer_own, layer_other, *own, *other)


def from_chips(value):
    count = lax.axis_size("dp")
    if count == 2:
        return [value, shift(value, "dp", 1)]
    gathered = lax.all_gather(value, "dp", axis=0, tiled=False)
    return [gathered[j] for j in range(count)]


def on_device(tokens, expert_ids, gates, out_grad, gate_weight, up_weight, down_weight):
    ids, gates, tokens, out_grad, gate_weight, up_weight, down_weight = (
        pltpu.with_memory_space_constraint(v, pltpu.HBM)
        for v in (expert_ids.T, gates.T, tokens, out_grad, gate_weight, up_weight, down_weight)
    )
    n = lax.axis_size("ed")
    slots = n * CAP
    half = tokens.shape[1] // 2
    hid = gate_weight.shape[1]

    (own_tok, own_grad, own_coef), sent, placing = pick(n, hid, ids, gates, tokens, out_grad)
    arrived = [shift(sent[s - 1], "ed", s) for s in range(1, n)]
    gate_held, gate_done = load(own_coef, gate_weight)
    up_held, up_done = load(gate_done, up_weight)
    direct = stack(up_done, arrived)
    other = shift(direct, "tp", 1)
    rows, hidden, act, slope = forward(n, own_tok, direct, other, gate_held, up_held)
    scaled, gate_pre, up_pre, router, out_part, out_keep = middle(
        n, own_grad, own_coef, direct, other, hidden, act, slope, down_weight
    )
    out_got = shift(out_part, "tp", 1)
    in_part = input_part(False, BF16, slots, gate_pre, up_pre, gate_held, up_held)
    in_got = shift(in_part, "tp", 1)
    in_keep = input_part(True, F32, slots, gate_pre, up_pre, gate_held, up_held)
    in_chunks = merge(router, range(n), in_keep, in_got, router)
    in_back = [in_chunks[0]] + [shift(in_chunks[s], "ed", -s) for s in range(1, n)]
    first, second, weighted = placing
    up_w_grad, done = weight_grad(in_chunks[0], rows, up_pre, "up_grad")
    out_chunks = merge(done, range(n), out_keep, out_got)
    out_back = [out_chunks[0]] + [shift(out_chunks[s], "ed", -s) for s in range(1, n)]
    in_mine = combine_router(done, n, first, second, in_back)
    gate_w_grad, done = weight_grad(in_mine, rows, gate_pre, "gate_grad")
    out_mine = combine(done, n, weighted, out_back)
    down_grad, done = weight_grad(out_mine, hidden, scaled, "down_grad")
    in_own = from_chips(in_mine)
    out_half = add_pieces(done, from_chips(out_mine))
    layer_out, token_grad, gate_grad = finish(
        half, out_half, shift(out_half, "tp", 1),
        in_own, [shift(piece, "tp", 1) for piece in in_own],
    )
    return layer_out, token_grad, gate_grad.T, gate_w_grad, up_w_grad, down_grad


def solution(mesh):
    token_spec = P(("groups", "ed"), None)
    in_specs = (
        token_spec,
        token_spec,
        token_spec,
        token_spec,
        P(None, ("ed", "dp", "tp")),
        P(None, ("ed", "dp", "tp")),
        P(("ed", "dp", "tp"), None),
    )
    out_specs = (
        token_spec,
        token_spec,
        token_spec,
        P("groups", ("ed", "dp", "tp")),
        P("groups", ("ed", "dp", "tp")),
        P(("groups", "ed", "dp", "tp"), None),
    )
    return jax.shard_map(
        on_device, mesh=mesh, in_specs=in_specs, out_specs=out_specs, check_vma=False
    )
```
